512 devices in a mesh: gx: 8 (over y, core), gy: 8 (over x, z_hi), gz: 8 (over z_lo).
Axes of the slice: x: 4, y: 4, z: 16 (z_hi: 2, z_lo: 8; z = z_hi * 8 + z_lo), core: 2. Of those that a mesh axis runs over, the one named last changes fastest.
Arguments:
- loads: float32 [8, 3, 32, 64, 1024], P(None, None, 'gx', 'gy', 'gz'), may hold values from -6 to 6
- iterate: float32 [8, 3, 32, 64, 1024], P(None, None, 'gx', 'gy', 'gz'), may hold values from -4 to 4
- classes: int32 [32, 64, 1024], P('gx', 'gy', 'gz'), may hold values from 0 to 7
- stiffness: float32 [8], replicated, may hold values from 0.5 to 5
- density: float32 [8], replicated, may hold values from 1 to 4
- basis: float32 [32, 3, 32, 64, 1024], P(None, None, 'gx', 'gy', 'gz'), may hold values from -0.625 to 0.625
- coarse_inverse: float32 [16384, 16384], P(('gx', 'gy', 'gz')), may hold values from -0.046875 to 0.046875
Outputs:
- updated: float32 [8, 3, 32, 64, 1024], P(None, None, 'gx', 'gy', 'gz')
The draws below stay inside these ranges and needn't reach their ends.
All inputs are finite; a program needn't handle non-finite values.
Results may differ from the reference program's by a relative error of at most 0.0003.
Values sent between devices are 32-bit elements; how exact they have to be, the bound alone decides.
A program may use at most 64 MiB of HBM per device.

```python
import math
import jax
import jax.numpy as jnp
from jax import lax

CX = 4
CY = 8
CZ = 128
COLS = 8
NB = 32
NCLASS = 8
SWEEPS = 4
NX = 32
NY = 64
NZ = 1024
NC = 16384
N_GX = 8
N_GY = 8
N_GZ = 8


def touch_ends(result, stream_key, smallest, largest):
    shape = result.shape
    index_at = [jax.random.randint(jax.random.fold_in(stream_key, axis), (), 0, shape[axis]) for axis in range(len(shape))]
    result = result.at[tuple(index_at)].set(smallest)
    longest = shape.index(max(shape))
    index_at[longest] = (index_at[longest] + 1) % shape[longest]
    return result.at[tuple(index_at)].set(largest)


def level_of(stream_key, extent, shards, smallest, largest):
    factor_of, own = 1.0, jax.random.fold_in(stream_key, 6)
    for axis_at, blocks in shards:
        steps = jnp.exp(jax.random.uniform(jax.random.fold_in(own, axis_at), (blocks,), jnp.float32, smallest / len(shards), largest / len(shards)))
        factor_of = factor_of * jnp.repeat(steps, extent[axis_at] // blocks).reshape([-1 if axis == axis_at else 1 for axis in range(len(extent))])
    return factor_of


def bell_draw(key, shape, width, limit, split=(), kind=jnp.bfloat16):
    result = jax.random.normal(key, shape, jnp.float32) * width
    if len(split) > 0:
        result = level_of(key, shape, split, -0.22, 0.18) * result
    return jnp.clip(result, min=-limit, max=limit).astype(kind)


def setup_inputs(seed: int = 0) -> dict:
    arg_keys = jax.random.split(jax.random.key(seed), 8)
    return {
        "loads": bell_draw(arg_keys[0], (COLS, 3, NX, NY, NZ), 1.0, 6.0, ((2, 8), (3, 8), (4, 8)), jnp.float32),
        "iterate": bell_draw(arg_keys[1], (COLS, 3, NX, NY, NZ), 0.3, 4.0, ((2, 8), (3, 8), (4, 8)), jnp.float32),
        "classes": touch_ends(jax.random.randint(arg_keys[2], (NX, NY, NZ), 0, NCLASS), jax.random.fold_in(arg_keys[2], 1), 0, NCLASS - 1).astype(jnp.int32),
        "stiffness": jnp.clip(jnp.exp(jax.random.uniform(arg_keys[3], (NCLASS,), jnp.float32, math.log(0.5), math.log(5.0))), 0.5, 5.0),
        "density": jnp.clip(jnp.exp(jax.random.uniform(arg_keys[4], (NCLASS,), jnp.float32, math.log(1.0), math.log(4.0))), 1.0, 4.0),
        "basis": bell_draw(arg_keys[5], (NB, 3, NX, NY, NZ), ((3 * CX * CY * CZ * NB) ** -0.25), 0.625, ((2, 8), (3, 8), (4, 8)), jnp.float32),
        "coarse_inverse": bell_draw(arg_keys[6], (NC, NC), NC ** -0.5, 0.046875, ((0, 512),), jnp.float32),
    }


coupling = 0.1
damping = 0.7


def lookup(classes, table):
    matches = classes[..., None] == jnp.arange(table.shape[0], dtype=jnp.int32)
    return jnp.sum(jnp.where(matches, table, jnp.float32(0.0)), axis=-1)


def stencil(padded, stiff_field, mass_field):
    center = padded[..., 1:-1, 1:-1, 1:-1]
    beside = padded[..., 2:, 1:-1, 1:-1] + padded[..., :-2, 1:-1, 1:-1]
    beside = beside + padded[..., 1:-1, 2:, 1:-1] + padded[..., 1:-1, :-2, 1:-1]
    beside = beside + padded[..., 1:-1, 1:-1, 2:] + padded[..., 1:-1, 1:-1, :-2]
    summed = jnp.sum(center, axis=1, keepdims=True)
    return (6.0 * stiff_field + mass_field) * center - stiff_field * beside + coupling * stiff_field * (summed - center)


def smooth(residual_ext, shifted_classes, stiffness, density):
    inside = shifted_classes > 0
    material = shifted_classes - 1
    stiff_field = lookup(material, stiffness)
    mass_field = lookup(material, density)
    diagonal = jnp.where(inside, 6.0 * stiff_field + mass_field - coupling * stiff_field, jnp.float32(1.0))
    update = jnp.zeros_like(residual_ext)
    for sweep in range(SWEEPS):
        padded = jnp.pad(update, ((0, 0), (0, 0), (1, 1), (1, 1), (1, 1)))
        update = jnp.where(inside, update + damping * (residual_ext - stencil(padded, stiff_field, mass_field)) / diagonal, jnp.float32(0.0))
    return update[..., 2:-2, 2:-2, 2:-2]


def reference(loads, iterate, classes, stiffness, density, basis, coarse_inverse):
    highest = lax.Precision.HIGHEST
    stiff_field = lookup(classes, stiffness)
    mass_field = lookup(classes, density)
    padded = jnp.pad(iterate, ((0, 0), (0, 0), (1, 1), (1, 1), (1, 1)))
    residual = loads - stencil(padded, stiff_field, mass_field)
    res_pad = jnp.pad(residual, ((0, 0), (0, 0), (2, 2), (2, 2), (2, 2)))
    class_pad = jnp.pad(classes + 1, 2)

    def starts(domain):
        index_x = domain // (N_GY * N_GZ)
        index_y = (domain // N_GZ) % N_GY
        index_z = domain % N_GZ
        return (index_x * CX).astype(jnp.int32), (index_y * CY).astype(jnp.int32), (index_z * CZ).astype(jnp.int32)

    def local(domain):
        start_x, start_y, start_z = starts(domain)
        zero = jnp.zeros((), jnp.int32)
        res_box = lax.dynamic_slice(res_pad, (zero, zero, start_x, start_y, start_z), (COLS, 3, CX + 4, CY + 4, CZ + 4))
        class_box = lax.dynamic_slice(class_pad, (start_x, start_y, start_z), (CX + 4, CY + 4, CZ + 4))
        own_basis = lax.dynamic_slice(basis, (zero, zero, start_x, start_y, start_z), (NB, 3, CX, CY, CZ))
        fine = smooth(res_box, class_box, stiffness, density)
        own_res = res_box[..., 2:-2, 2:-2, 2:-2]
        coeff = jnp.dot(own_basis.reshape(NB, -1), own_res.reshape(COLS, -1).T, precision=highest)
        return fine, coeff

    domains = jnp.arange(N_GX * N_GY * N_GZ, dtype=jnp.int32)
    fines, coeffs = lax.map(local, domains)
    solved = jnp.dot(coarse_inverse, coeffs.reshape(-1, COLS), precision=highest)

    def decode(pair):
        domain, fine = pair
        start_x, start_y, start_z = starts(domain)
        zero = jnp.zeros((), jnp.int32)
        own_basis = lax.dynamic_slice(basis, (zero, zero, start_x, start_y, start_z), (NB, 3, CX, CY, CZ))
        own_iter = lax.dynamic_slice(iterate, (zero, zero, start_x, start_y, start_z), (COLS, 3, CX, CY, CZ))
        block = lax.dynamic_slice_in_dim(solved, (domain * NB).astype(jnp.int32), NB, 0)
        correction = jnp.dot(block.T, own_basis.reshape(NB, -1), precision=highest).reshape(COLS, 3, CX, CY, CZ)
        return own_iter + fine + correction

    boxes = lax.map(decode, (domains, fines))
    boxes = boxes.reshape(N_GX, N_GY, N_GZ, COLS, 3, CX, CY, CZ)
    boxes = jnp.transpose(boxes, (3, 4, 0, 5, 1, 6, 2, 7))
    return boxes.reshape(COLS, 3, NX, NY, NZ)
```

```python
import functools

import jax
import jax.numpy as jnp
from jax import lax
from jax.experimental import pallas as pl
from jax.experimental.pallas import tpu as pltpu
from jax.sharding import PartitionSpec as P

MESH = pl.DeviceIdType.MESH
F32, BF16, I32 = jnp.float32, jnp.bfloat16, jnp.int32
FIELDS = 24
CHUNKS, PER = 4, 6
COUPLING, DAMPING = 0.1, 0.7
NT = (((1,), (1,)), ((), ()))


def lookup(classes, table):
    found = jnp.zeros(classes.shape, F32)
    for k in range(8):
        found = found + jnp.where(classes == k, table[k], 0.0)
    return found


def halves(v):
    high = v.astype(BF16)
    return high, (v - high.astype(F32)).astype(BF16)


def iota(shape, axis):
    return lax.broadcasted_iota(I32, shape, axis)


def beside_x(v, axis):
    row = iota(v.shape, axis)
    return jnp.where(row == 0, 0.0, pltpu.roll(v, 1, axis)) + jnp.where(row == 7, 0.0, pltpu.roll(v, 7, axis))


def kernel(
    ny, nx, nz, loads, iterate, classes, stiffness, density, basis, cinv, out,
    it, ld, acc, cls, bas, ci, res, iys, iyr, ixs, ixr, izs, izr, cbox, czs, czr, box, ys, yr,
    zs, zr, bt, c2, g1, g2, sbox, wbox, bbox, zw, zb, ga, gb, gc, za, zc, zd, vy,
    ss, rs, ls,
):
    gx, gy, gz = lax.axis_index("gx"), lax.axis_index("gy"), lax.axis_index("gz")
    half = nz // 2
    py, core, px, pz = gx // 2, gx % 2, gy // 2, (gy % 2) * half + gz

    def chip(x, y, z, c):
        return (y * 2 + c, x * 2 + z // half, z % half)

    steps = {
        "gx": ((gx - 1, gy, gz), gx > 0, (gx + 1, gy, gz), gx < 2 * ny - 1),
        "gy": ((gx, gy - 1, gz), gy > 0, (gx, gy + 1, gz), gy < 2 * nx - 1),
        "gz": ((gx, gy, gz - 1), gz > 0, (gx, gy, gz + 1), gz < half - 1),
    }
    count = [0]
    pending = []

    def exchange(axis, low_src, low_dst, high_src, high_dst):
        lower, has_lower, upper, has_upper = steps[axis]
        i = count[0]
        count[0] += 2
        down = pltpu.make_async_remote_copy(low_src, low_dst, ss.at[i], rs.at[i], lower, MESH)
        up = pltpu.make_async_remote_copy(high_src, high_dst, ss.at[i + 1], rs.at[i + 1], upper, MESH)
        pl.when(has_lower)(down.start)
        pl.when(has_upper)(up.start)

        def sent():
            pl.when(has_lower)(down.wait_send)
            pl.when(has_upper)(up.wait_send)

        def arrived():
            pl.when(has_upper)(down.wait_recv)
            pl.when(has_lower)(up.wait_recv)

        pending.append(sent)
        return arrived

    local = [
        pltpu.make_async_copy(a, b, ls.at[i])
        for i, (a, b) in enumerate(((iterate, it), (classes, cls), (loads, ld), (basis, bas), (cinv, ci)))
    ]
    for copy in local:
        copy.start()

    for ref in (iyr, ixr, izr, cbox, czr, box, yr, zr):
        ref[...] = jnp.zeros(ref.shape, ref.dtype)

    barrier = pltpu.get_barrier_semaphore()
    high_half = gy % 2
    across_gx = jnp.where(core == 1, gx < 2 * ny - 1, gx > 0)
    across_gy = jnp.where(high_half == 1, gy < 2 * nx - 1, gy > 0)
    for there, to in ((across_gx, (gx + 2 * core - 1, gy, gz)), (across_gy, (gx, gy + 2 * high_half - 1, gz))):
        pl.when(there)(functools.partial(pl.semaphore_signal, barrier, inc=1, device_id=to, device_id_type=MESH))

    def greet_line(k, carry):
        pl.semaphore_signal(barrier, inc=1, device_id=chip(px, py, lax.rem(pz + k, nz), core), device_id_type=MESH)
        return carry

    lax.fori_loop(1, nz, greet_line, 0)

    def other(p, sign):
        dx, dy = p // ny, lax.rem(p, ny)
        return lax.rem(px + sign * dx + nx, nx), lax.rem(py + sign * dy + ny, ny)

    def greet_plane(p, carry):
        x, y = other(p, 1)
        pl.semaphore_signal(barrier, inc=1, device_id=chip(x, y, pz, core), device_id_type=MESH)
        return carry

    lax.fori_loop(1, nx * ny, greet_plane, 0)
    twin = chip(px, py, pz, 1 - core)
    pl.semaphore_signal(barrier, inc=1, device_id=twin, device_id_type=MESH)

    lane8 = iota((8, 128), 1)
    sub8 = iota((8, 128), 0)

    local[0].wait()
    iys[0] = it[pl.ds(0, 96, stride=8), :]
    iys[1] = it[pl.ds(7, 96, stride=8), :]

    def pack_iterate(f, carry):
        low, high = carry
        start = pl.multiple_of(f * 32, 32)
        ixs[0, f] = it[pl.ds(start, 8), :]
        ixs[1, f] = it[pl.ds(start + 24, 8), :]
        for x in range(4):
            v = it[pl.ds(start + x * 8, 8), :]
            t = x * 32 + f
            low = jnp.where(lane8 == t, pltpu.roll(v, t, 1), low)
            high = jnp.where(lane8 == t, pltpu.roll(v, t + 1, 1), high)
        return low, high

    zero8 = jnp.zeros((8, 128), F32)
    low, high = lax.fori_loop(0, FIELDS, pack_iterate, (zero8, zero8), unroll=2)
    izs[0] = low
    izs[1] = high
    local[1].wait()
    for y in range(8):
        cbox[y + 2, 2:6] = cls[pl.ds(y, 4, stride=8), :] + 1

    acc[...] = it[...]
    for ref in (ga, gb, gc):
        ref[:, 0] = jnp.zeros((PER, 8, 128), F32)
        ref[:, 13] = jnp.zeros((PER, 8, 128), F32)
    for ref in (za, zc, zd):
        ref[0] = zero8
        ref[13] = zero8

    peers = nz - 1 + nx * ny - 1 + 1 + across_gx.astype(I32) + across_gy.astype(I32)
    pl.semaphore_wait(barrier, peers)

    cls_y = exchange("gy", cbox.at[2:4, 2:6], cbox.at[10:12, 2:6], cbox.at[8:10, 2:6], cbox.at[0:2, 2:6])
    it_y = exchange("gy", iys.at[0], iyr.at[1], iys.at[1], iyr.at[0])
    it_x = exchange("gx", ixs.at[0], ixr.at[1], ixs.at[1], ixr.at[0])
    it_z = exchange("gz", izs.at[0], izr.at[1], izs.at[1], izr.at[0])

    local[2].wait()

    def own_class(x):
        return cls[pl.ds(x * 8, 8), :]

    stiff_own = jnp.stack([lookup(own_class(x), stiffness) for x in range(4)])
    mass_own = jnp.stack([lookup(own_class(x), density) for x in range(4)])
    diag_own = 6.0 * stiff_own + mass_own - COUPLING * stiff_own

    it_x()
    it_z()

    def own_residual(col, carry):
        start = pl.multiple_of(col * 96, 96)
        u = it[pl.ds(start, 96), :].reshape(3, 4, 8, 128)
        lower = ixr[0, pl.ds(col * 3, 3)][:, None]
        upper = ixr[1, pl.ds(col * 3, 3)][:, None]
        near = jnp.concatenate([lower, u[:, :3]], 1) + jnp.concatenate([u[:, 1:], upper], 1)
        near = near + beside_x(u, 2)
        fill_low, fill_high = [], []
        for c in range(3):
            for x in range(4):
                t = x * 32 + col * 3 + c
                fill_low.append(pltpu.roll(izr[0], lax.rem(128 - t, 128), 1))
                fill_high.append(pltpu.roll(izr[1], 127 - t, 1))
        lane = iota(u.shape, 3)
        near = near + jnp.where(lane == 0, jnp.stack(fill_low).reshape(u.shape), pltpu.roll(u, 1, 3))
        near = near + jnp.where(lane == 127, jnp.stack(fill_high).reshape(u.shape), pltpu.roll(u, 127, 3))
        total = (u[0] + u[1] + u[2])[None]
        r = ld[pl.ds(start, 96), :].reshape(3, 4, 8, 128)
        r = r - diag_own[None] * u + stiff_own[None] * (near - COUPLING * total)
        res[pl.ds(start, 96), :] = r.reshape(96, 128)
        return carry

    lax.fori_loop(0, 8, own_residual, 0)

    def pack_rows(f, carry):
        for side in range(2):
            for layer in range(2):
                ys[side, f, layer * 4 : layer * 4 + 4] = res[pl.ds(f * 32 + side * 6 + layer, 4, stride=8), :]
        return carry

    lax.fori_loop(0, FIELDS, pack_rows, 0, unroll=2)
    res_y = []
    for ch in range(CHUNKS):
        fs = pl.ds(ch * PER, PER)
        res_y.append(exchange("gy", ys.at[0, fs], yr.at[1, fs], ys.at[1, fs], yr.at[0, fs]))

    local[3].wait()

    def prepare_basis(k, carry):
        hi, lo = halves(bas[pl.ds(k, 32, stride=96), :])
        at = pl.ds(pl.multiple_of(k * 128, 128), 128)
        bt[0:32, at] = hi
        bt[32:64, at] = lo
        bt[64:96, at] = hi
        bt[96:128, at] = jnp.zeros((32, 128), BF16)
        return carry

    lax.fori_loop(0, 96, prepare_basis, 0, unroll=2)

    def two(v):
        hi, lo = halves(v)
        return jnp.concatenate([hi, lo], 0)

    def coefficients(k, total):
        v = jnp.concatenate([res[pl.ds(k * 8 + i, 8, stride=96), :] for i in range(8)], 1)
        at = pl.ds(pl.multiple_of(k * 1024, 1024), 1024)
        return total + lax.dot_general(two(v), bt[0:64, at], NT, preferred_element_type=F32)

    coeff = lax.fori_loop(0, 12, coefficients, jnp.zeros((16, 64), F32))

    local[4].wait()

    def prepare_coarse(k, carry):
        at = pl.ds(pl.multiple_of(k * 512, 512), 512)
        hi, lo = halves(ci[:, at])
        c2[0:32, at] = hi
        c2[32:64, at] = lo
        return carry

    lax.fori_loop(0, ci.shape[1] // 512, prepare_coarse, 0)

    cls_y()
    cls_x = exchange("gx", cbox.at[:, 2:4], cbox.at[:, 6:8], cbox.at[:, 4:6], cbox.at[:, 0:2])
    cls_x()
    low = jnp.zeros((8, 128), I32)
    high = jnp.zeros((8, 128), I32)
    for y in range(12):
        mask = lane8 // 2 == y
        low = jnp.where(mask, pltpu.roll(cbox[y], 2 * y, 1), low)
        high = jnp.where(mask, pltpu.roll(cbox[y], 2 * y + 2, 1), high)
    czs[0] = low
    czs[1] = high
    cls_z = exchange("gz", czs.at[0], czr.at[1], czs.at[1], czr.at[0])
    cls_z()

    def factors(shifted):
        inside = shifted > 0
        stiff = lookup(shifted - 1, stiffness)
        mass = lookup(shifted - 1, density)
        weight = jnp.where(inside, DAMPING / jnp.where(inside, 6.0 * stiff + mass - COUPLING * stiff, 1.0), 0.0)
        return stiff, weight

    def box_factors(y, carry):
        stiff, weight = factors(cbox[y])
        sbox[y] = stiff
        wbox[y] = weight
        bbox[y] = stiff * weight
        base = lane8 % 2
        spread = jnp.zeros((8, 128), I32)
        for side in range(2):
            two_lanes = jnp.where(lane8 < 2, pltpu.roll(czr[side], 128 - 2 * y, 1), 0)
            pair = two_lanes + pltpu.roll(two_lanes, 2, 1)
            six = pair + pltpu.roll(pair, 4, 1) + pltpu.roll(pair, 8, 1)
            spread = spread + (six if side == 0 else pltpu.roll(six, 12, 1))
        stiff, weight = factors(spread)
        zw[y] = weight
        zb[y] = stiff * weight
        return carry

    lax.fori_loop(0, 12, box_factors, 0)

    it_y()
    parts, columns = [], []
    for side in range(2):
        row = cls[pl.ds(side * 7, 4, stride=8), :]
        stiff = lookup(jnp.concatenate([row, row], 0), stiffness)
        v = (iyr[side].reshape(12, 8, 128) * stiff[None]).reshape(96, 128)
        vy[side] = v
        res[pl.ds(side * 7, 96, stride=8), :] = res[pl.ds(side * 7, 96, stride=8), :] + v
    for side in range(2):
        for cx in range(12):
            k = cx * 8 + side * 7
            parts.append(vy[side, pl.ds(cx, 8, stride=12), :])
            columns.append(bt[0:64, k * 128 : k * 128 + 128])
    coeff = coeff + lax.dot_general(
        two(jnp.concatenate(parts, 1)), jnp.concatenate(columns, 1), NT, preferred_element_type=F32
    )

    def quarters(v):
        v = v[0:8] + v[8:16]
        v = v[:, 0:32] + v[:, 32:64]
        return jnp.concatenate([v, jnp.zeros((8, 96), F32)], 1)

    mine = quarters(coeff)
    packed = zero8
    for q in range(4):
        v = pltpu.roll(mine, 32 * q, 1) if q else mine
        v = pltpu.roll(v, 8 - q, 0) if q else v
        packed = jnp.where(lane8 // 32 == q, v, packed)
    g1[pz, 0:1] = packed[0:1]
    g1[pz, 1:2] = packed[4:5]
    line = count[0]
    count[0] += nz
    plane = count[0]
    count[0] += nx * ny
    twins = count[0]
    count[0] += nx * ny

    def along_line(k):
        to = chip(px, py, lax.rem(pz + k, nz), core)
        return pltpu.make_async_remote_copy(g1.at[pz], g1.at[pz], ss.at[line + k], rs.at[line + k], to, MESH)

    def start_line(k, carry):
        along_line(k).start()
        return carry

    lax.fori_loop(1, nz, start_line, 0)

    def own_rows(f, carry):
        for y in range(8):
            box[f, y + 2, 2:6] = res[pl.ds(f * 32 + y, 4, stride=8), :]
        return carry

    lax.fori_loop(0, FIELDS, own_rows, 0, unroll=2)
    own_x = exchange("gx", box.at[:, 2:10, 2:4], box.at[:, 2:10, 6:8], box.at[:, 2:10, 4:6], box.at[:, 2:10, 0:2])

    res_x, res_z = {}, {}

    def rows_arrive(ch):
        res_y[ch]()
        fs = pl.ds(ch * PER, PER)
        _, has_lower, _, has_upper = steps["gy"]

        @pl.when(has_lower)
        def _():
            for f in range(ch * PER, ch * PER + PER):
                v = yr[0, f]
                box[f, 0, 2:6] = v[0:4]
                box[f, 1, 2:6] = v[4:8] + sbox[1, 2:6] * iys[0, f * 4 : f * 4 + 4]

        @pl.when(has_upper)
        def _():
            for f in range(ch * PER, ch * PER + PER):
                v = yr[1, f]
                box[f, 10, 2:6] = v[0:4] + sbox[10, 2:6] * iys[1, f * 4 : f * 4 + 4]
                box[f, 11, 2:6] = v[4:8]

        first = exchange("gx", box.at[fs, 0:2, 2:4], box.at[fs, 0:2, 6:8], box.at[fs, 0:2, 4:6], box.at[fs, 0:2, 0:2])
        second = exchange(
            "gx", box.at[fs, 10:12, 2:4], box.at[fs, 10:12, 6:8], box.at[fs, 10:12, 4:6], box.at[fs, 10:12, 0:2]
        )
        res_x[ch] = (first, second)

    def planes_arrive(ch):
        if ch == 0:
            own_x()
        for arrived in res_x[ch]:
            arrived()
        lane = iota((12, 8, 128), 2)
        low = jnp.zeros((12, 8, 128), F32)
        high = jnp.zeros((12, 8, 128), F32)
        for i in range(PER):
            v = box[ch * PER + i]
            mask = lane // 2 == i
            low = jnp.where(mask, pltpu.roll(v, 2 * i, 2) if i else v, low)
            high = jnp.where(mask, pltpu.roll(v, 2 * i + 2, 2), high)
        for side, v in enumerate((low, high)):
            first, second = zero8, zero8
            for y in range(12):
                t = (y % 10) * 12
                w = pltpu.roll(v[y], t, 1) if t else v[y]
                if y < 10:
                    first = first + w
                else:
                    second = second + w
            zs[ch, side, 0] = first
            zs[ch, side, 1] = second
        res_z[ch] = exchange("gz", zs.at[ch, 0], zr.at[ch, 1], zs.at[ch, 1], zr.at[ch, 0])

    def sweep(src, zsrc, dst, zdst, y):
        e, z = src[:, y], zsrc[y]
        lane, lane6 = lane8, iota((PER, 8, 128), 2)
        near = src[:, y - 1] + src[:, y + 1] + beside_x(e, 1)
        fill_low = jnp.stack([pltpu.roll(z, 127 - 2 * i, 1) for i in range(PER)])
        fill_high = jnp.stack([pltpu.roll(z, 115 - 2 * i, 1) for i in range(PER)])
        near = near + jnp.where(lane6 == 0, fill_low, pltpu.roll(e, 1, 2))
        near = near + jnp.where(lane6 == 127, fill_high, pltpu.roll(e, 127, 2))
        totals = jnp.stack([e[0] + e[1] + e[2]] * 3 + [e[3] + e[4] + e[5]] * 3)
        dst_value = ga[:, y] + (1.0 - DAMPING) * e + bbox[y - 1][None] * (near - COUPLING * totals)
        if zdst is not None:
            dst[:, y] = dst_value
            push = jnp.zeros((8, 128), F32)
            for i in range(PER):
                push = jnp.where(lane == 2 * i + 1, pltpu.roll(e[i], 2 * i + 1, 1), push)
                push = jnp.where(lane == 12 + 2 * i, pltpu.roll(e[i], 13 + 2 * i, 1), push)
            back, ahead = pltpu.roll(z, 1, 1), pltpu.roll(z, 127, 1)
            znear = zsrc[y - 1] + zsrc[y + 1] + beside_x(z, 0) + push + jnp.where(lane % 2 == 0, ahead, back)
            two_on, four_on = pltpu.roll(z, 126, 1), pltpu.roll(z, 124, 1)
            two_back, four_back = pltpu.roll(z, 2, 1), pltpu.roll(z, 4, 1)
            comp = (lane // 2) % 3
            rest = jnp.where(
                comp == 0, two_on + four_on, jnp.where(comp == 1, two_on + two_back, two_back + four_back)
            )
            zdst[y] = za[y] + (1.0 - DAMPING) * z + zb[y - 1] * (znear - COUPLING * (z + rest))
        return dst_value

    def sweeps(ch):
        res_z[ch]()

        def start(y, carry):
            ga[:, y + 1] = box[pl.ds(ch * PER, PER), y] * wbox[y][None]
            return carry

        lax.fori_loop(0, 12, start, 0)
        for y in range(12):
            t = (y % 10) * 12
            low, high = zr[ch, 0, y // 10], zr[ch, 1, y // 10]
            low = pltpu.roll(low, 128 - t, 1) if t else low
            high = pltpu.roll(high, (140 - t) % 128, 1) if t != 12 else high
            z = jnp.where(lane8 < 12, low, jnp.where(lane8 < 24, high, 0.0))
            za[y + 1] = z * zw[y]

        def first(y, carry):
            sweep(ga, za, gb, zc, y)
            return carry

        lax.fori_loop(1, 13, first, 0)

        def second(y, carry):
            sweep(gb, zc, gc, zd, y)
            return carry

        lax.fori_loop(2, 12, second, 0)

        def third(y, carry):
            v = sweep(gc, zd, None, None, y)
            for i in range(PER):
                at = pl.ds((ch * PER + i) * 32 + y - 3, 4, stride=8)
                acc[at, :] = acc[at, :] + v[i, 2:6]
            return carry

        lax.fori_loop(3, 11, third, 0)

    def block(x, y, c):
        return (y * 2 + c) * nx + x

    def along_plane(p):
        x, y = other(p, 1)
        b = block(px, py, core)
        return pltpu.make_async_remote_copy(
            g2.at[b], g2.at[b], ss.at[plane + p], rs.at[plane + p], chip(x, y, pz, core), MESH
        )

    def to_twin(p):
        x, y = other(p, -1)
        b = block(x, y, core)
        return pltpu.make_async_remote_copy(g2.at[b], g2.at[b], ss.at[twins + p], rs.at[twins + p], twin, MESH)

    def line_arrives():
        def arrive(k, carry):
            along_line(k).wait_recv()
            return carry

        lax.fori_loop(1, nz, arrive, 0)
        groups = nz // 4
        rows = g1[...]
        upper = jnp.broadcast_to(rows[:, 0:1], (nz, 8, 128))
        lower = jnp.broadcast_to(rows[:, 1:2], (nz, 8, 128))
        both = jnp.where(iota((nz, 8, 128), 1) < 4, upper, lower).reshape(groups, 4, 8, 128)
        lane, sub = iota((groups, 8, 128), 2) // 32, iota((groups, 8, 128), 1) % 4
        spread = jnp.zeros((groups, 8, 128), F32)
        for zz in range(4):
            for q in range(4):
                t = 32 * ((zz - q) % 4)
                v = both[:, zz]
                v = pltpu.roll(v, t, 2) if t else v
                spread = jnp.where((lane == zz) & (sub == q), v, spread)
        b = block(px, py, core)
        g2[b] = jnp.concatenate([spread[i] for i in range(groups)], 1)

        def start(p, carry):
            along_plane(p).start()
            return carry

        lax.fori_loop(1, nx * ny, start, 0)
        to_twin(0).start()

    width = nz * 32

    def times_block(b, total):
        at = pl.ds(pl.multiple_of(b * width, width), width)
        return total + lax.dot_general(two(g2[b]), c2[:, at], NT, preferred_element_type=F32)

    def plane_arrives():
        def arrive(p, total):
            along_plane(p).wait_recv()
            to_twin(p).start()
            x, y = other(p, -1)
            return times_block(block(x, y, core), total)

        return lax.fori_loop(1, nx * ny, arrive, times_block(block(px, py, core), jnp.zeros((16, 64), F32)))

    def twins_arrive(total):
        def arrive(p, total):
            to_twin(p).wait_recv()
            x, y = other(p, -1)
            return times_block(block(x, y, 1 - core), total)

        total = lax.fori_loop(0, nx * ny, arrive, total)
        solved = quarters(total)
        hi = solved.astype(BF16).astype(F32)
        lo = solved - hi
        factor = hi + pltpu.roll(hi, 32, 1) + pltpu.roll(lo, 64, 1)
        factor = factor.astype(BF16)

        def correct(k, carry):
            at = pl.ds(pl.multiple_of(k * 1024, 1024), 1024)
            v = jnp.dot(factor, bt[:, at], preferred_element_type=F32)
            for i in range(8):
                rows = pl.ds(k * 8 + i, 8, stride=96)
                acc[rows, :] = acc[rows, :] + v[:, i * 128 : i * 128 + 128]
            return carry

        lax.fori_loop(0, 12, correct, 0)

    rows_arrive(0)
    line_arrives()
    rows_arrive(1)
    planes_arrive(0)
    rows_arrive(2)
    planes_arrive(1)
    sweeps(0)
    total = plane_arrives()
    rows_arrive(3)
    planes_arrive(2)
    sweeps(1)
    planes_arrive(3)
    twins_arrive(total)
    sweeps(2)
    sweeps(3)
    done = pltpu.make_async_copy(acc, out, ls.at[5])
    done.start()

    for sent in pending:
        sent()

    def all_sent(k, carry):
        along_line(k).wait_send()
        return carry

    lax.fori_loop(1, nz, all_sent, 0)

    def all_sent_plane(p, carry):
        along_plane(p).wait_send()
        to_twin(p).wait_send()
        return carry

    to_twin(0).wait_send()
    lax.fori_loop(1, nx * ny, all_sent_plane, 0)
    done.wait()


def solution(mesh):
    ny, nx, nz = mesh.shape["gx"] // 2, mesh.shape["gy"] // 2, mesh.shape["gz"] * 2
    nc = 2 * ny * nx * nz * 32

    def step(loads, iterate, classes, stiffness, density, basis, coarse_inverse):
        v = pltpu.VMEM
        scratch = [
            v((768, 128), F32), v((768, 128), F32), v((768, 128), F32), v((32, 128), I32), v((3072, 128), F32),
            v((32, nc), F32), v((768, 128), F32),
            v((2, 96, 128), F32), v((2, 96, 128), F32), v((2, FIELDS, 8, 128), F32), v((2, FIELDS, 8, 128), F32),
            v((2, 8, 128), F32), v((2, 8, 128), F32),
            v((12, 8, 128), I32), v((2, 8, 128), I32), v((2, 8, 128), I32),
            v((FIELDS, 12, 8, 128), F32), v((2, FIELDS, 8, 128), F32), v((2, FIELDS, 8, 128), F32),
            v((CHUNKS, 2, 2, 8, 128), F32), v((CHUNKS, 2, 2, 8, 128), F32),
            v((128, 12288), BF16), v((64, nc), BF16),
            v((nz, 2, 128), F32), v((2 * ny * nx, 8, nz * 32), F32),
            v((12, 8, 128), F32), v((12, 8, 128), F32), v((12, 8, 128), F32), v((12, 8, 128), F32),
            v((12, 8, 128), F32),
            v((PER, 14, 8, 128), F32), v((PER, 14, 8, 128), F32), v((PER, 14, 8, 128), F32),
            v((14, 8, 128), F32), v((14, 8, 128), F32), v((14, 8, 128), F32),
            v((2, 96, 128), F32),
            pltpu.SemaphoreType.DMA((128,)), pltpu.SemaphoreType.DMA((128,)), pltpu.SemaphoreType.DMA((6,)),
        ]
        hbm, smem = pl.BlockSpec(memory_space=pl.ANY), pl.BlockSpec(memory_space=pltpu.SMEM)
        result = pl.pallas_call(
            functools.partial(kernel, ny, nx, nz),
            out_shape=jax.ShapeDtypeStruct((768, 128), F32),
            in_specs=[hbm, hbm, hbm, smem, smem, hbm, hbm],
            out_specs=hbm,
            scratch_shapes=scratch,
            compiler_params=pltpu.CompilerParams(
                collective_id=0, has_side_effects=True, vmem_limit_bytes=48 * 1024 * 1024
            ),
            name="schwarz",
        )(
            loads.reshape(768, 128), iterate.reshape(768, 128), classes.reshape(32, 128), stiffness, density,
            basis.reshape(3072, 128), coarse_inverse,
        )
        return result.reshape(iterate.shape)

    field = P(None, None, "gx", "gy", "gz")
    return jax.shard_map(
        step,
        mesh=mesh,
        in_specs=(field, field, P("gx", "gy", "gz"), P(), P(), field, P(("gx", "gy", "gz"), None)),
        out_specs=field,
        check_vma=False,
    )
```

```python
import functools

import jax
import jax.numpy as jnp
from jax import lax
from jax.experimental import pallas as pl
from jax.experimental.pallas import tpu as pltpu
from jax.sharding import PartitionSpec as P

MESH = pl.DeviceIdType.MESH
F32, BF16, I32 = jnp.float32, jnp.bfloat16, jnp.int32
FIELDS = 24
CHUNKS, PER = 4, 6
COUPLING, DAMPING = 0.1, 0.7
NT = (((1,), (1,)), ((), ()))


def lookup(classes, table):
    found = jnp.zeros(classes.shape, F32)
    for k in range(8):
        found = found + jnp.where(classes == k, table[k], 0.0)
    return found


def halves(v):
    high = v.astype(BF16)
    return high, (v - high.astype(F32)).astype(BF16)


def iota(shape, axis):
    return lax.broadcasted_iota(I32, shape, axis)


def beside_x(v, axis):
    row = iota(v.shape, axis)
    return jnp.where(row == 0, 0.0, pltpu.roll(v, 1, axis)) + jnp.where(row == 7, 0.0, pltpu.roll(v, 7, axis))


def kernel(
    ny, nx, nz, loads, iterate, classes, stiffness_in, density_in, basis, cinv, acc,
    it, ld, cls, stiffness, density, bas, ci, res, iys, iyr, ixs, ixr, izs, izr, cbox, czs, czr, box, ys, yr,
    zs, zr, bh, bl, bf, c2, g1, g2, sbox, wbox, bbox, zw, zb, ga, gb, gc, za, zc, zd, vy,
    ss, rs, ls,
):
    gx, gy, gz = lax.axis_index("gx"), lax.axis_index("gy"), lax.axis_index("gz")
    half = nz // 2
    py, core, px, pz = gx // 2, gx % 2, gy // 2, (gy % 2) * half + gz

    def chip(x, y, z, c):
        return (y * 2 + c, x * 2 + z // half, z % half)

    steps = {
        "gx": ((gx - 1, gy, gz), gx > 0, (gx + 1, gy, gz), gx < 2 * ny - 1),
        "gy": ((gx, gy - 1, gz), gy > 0, (gx, gy + 1, gz), gy < 2 * nx - 1),
        "gz": ((gx, gy, gz - 1), gz > 0, (gx, gy, gz + 1), gz < half - 1),
    }
    count = [0]
    pending = []

    def exchange(axis, low_src, low_dst, high_src, high_dst):
        lower, has_lower, upper, has_upper = steps[axis]
        i = count[0]
        count[0] += 2
        down = pltpu.make_async_remote_copy(low_src, low_dst, ss.at[i], rs.at[i], lower, MESH)
        up = pltpu.make_async_remote_copy(high_src, high_dst, ss.at[i + 1], rs.at[i + 1], upper, MESH)
        pl.when(has_lower)(down.start)
        pl.when(has_upper)(up.start)

        def sent():
            pl.when(has_lower)(down.wait_send)
            pl.when(has_upper)(up.wait_send)

        def arrived():
            pl.when(has_upper)(down.wait_recv)
            pl.when(has_lower)(up.wait_recv)

        pending.append(sent)
        return arrived

    local = [
        pltpu.make_async_copy(a, b, ls.at[i])
        for i, (a, b) in enumerate(
            (
                (iterate, it), (classes, cls), (loads, ld), (basis, bas), (cinv, ci),
                (stiffness_in, stiffness), (density_in, density),
            )
        )
    ]
    for copy in local:
        copy.start()

    for ref in (iyr, ixr, izr, cbox, czr, box, yr, zr):
        ref[...] = jnp.zeros(ref.shape, ref.dtype)

    barrier = pltpu.get_barrier_semaphore()
    high_half = gy % 2
    across_gx = jnp.where(core == 1, gx < 2 * ny - 1, gx > 0)
    across_gy = jnp.where(high_half == 1, gy < 2 * nx - 1, gy > 0)
    for there, to in ((across_gx, (gx + 2 * core - 1, gy, gz)), (across_gy, (gx, gy + 2 * high_half - 1, gz))):
        pl.when(there)(functools.partial(pl.semaphore_signal, barrier, inc=1, device_id=to, device_id_type=MESH))

    def greet_line(k, carry):
        pl.semaphore_signal(barrier, inc=1, device_id=chip(px, py, lax.rem(pz + k, nz), core), device_id_type=MESH)
        return carry

    lax.fori_loop(1, nz, greet_line, 0)

    def other(p, sign):
        dx, dy = p // ny, lax.rem(p, ny)
        return lax.rem(px + sign * dx + nx, nx), lax.rem(py + sign * dy + ny, ny)

    def greet_plane(p, carry):
        x, y = other(p, 1)
        pl.semaphore_signal(barrier, inc=1, device_id=chip(x, y, pz, core), device_id_type=MESH)
        return carry

    lax.fori_loop(1, nx * ny, greet_plane, 0)
    twin = chip(px, py, pz, 1 - core)
    pl.semaphore_signal(barrier, inc=1, device_id=twin, device_id_type=MESH)

    lane8 = iota((8, 128), 1)
    sub8 = iota((8, 128), 0)

    local[0].wait()
    iys[0] = it[pl.ds(0, 96, stride=8), :]
    iys[1] = it[pl.ds(7, 96, stride=8), :]

    def pack_iterate(f, carry):
        low, high = carry
        start = pl.multiple_of(f * 32, 32)
        ixs[0, f] = it[pl.ds(start, 8), :]
        ixs[1, f] = it[pl.ds(start + 24, 8), :]
        for x in range(4):
            v = it[pl.ds(start + x * 8, 8), :]
            t = x * 32 + f
            low = jnp.where(lane8 == t, pltpu.roll(v, t, 1), low)
            high = jnp.where(lane8 == t, pltpu.roll(v, t + 1, 1), high)
        return low, high

    zero8 = jnp.zeros((8, 128), F32)
    low, high = lax.fori_loop(0, FIELDS, pack_iterate, (zero8, zero8), unroll=2)
    izs[0] = low
    izs[1] = high
    local[1].wait()
    for y in range(8):
        cbox[y + 2, 2:6] = cls[pl.ds(y, 4, stride=8), :] + 1

    acc[...] = it[...]
    for ref in (ga, gb, gc):
        ref[:, 0] = jnp.zeros((PER, 8, 128), F32)
        ref[:, 13] = jnp.zeros((PER, 8, 128), F32)
    for ref in (za, zc, zd):
        ref[0] = zero8
        ref[13] = zero8

    peers = nz - 1 + nx * ny - 1 + 1 + across_gx.astype(I32) + across_gy.astype(I32)
    pl.semaphore_wait(barrier, peers)

    cls_y = exchange("gy", cbox.at[2:4, 2:6], cbox.at[10:12, 2:6], cbox.at[8:10, 2:6], cbox.at[0:2, 2:6])
    it_y = exchange("gy", iys.at[0], iyr.at[1], iys.at[1], iyr.at[0])
    it_x = exchange("gx", ixs.at[0], ixr.at[1], ixs.at[1], ixr.at[0])
    it_z = exchange("gz", izs.at[0], izr.at[1], izs.at[1], izr.at[0])

    local[5].wait()
    local[6].wait()
    local[2].wait()

    def own_class(x):
        return cls[pl.ds(x * 8, 8), :]

    stiff_own = jnp.stack([lookup(own_class(x), stiffness) for x in range(4)])
    mass_own = jnp.stack([lookup(own_class(x), density) for x in range(4)])
    diag_own = 6.0 * stiff_own + mass_own - COUPLING * stiff_own

    it_x()
    it_z()

    def own_residual(col, carry):
        start = pl.multiple_of(col * 96, 96)
        u = it[pl.ds(start, 96), :].reshape(3, 4, 8, 128)
        lower = ixr[0, pl.ds(col * 3, 3)][:, None]
        upper = ixr[1, pl.ds(col * 3, 3)][:, None]
        near = jnp.concatenate([lower, u[:, :3]], 1) + jnp.concatenate([u[:, 1:], upper], 1)
        near = near + beside_x(u, 2)
        fill_low, fill_high = [], []
        for c in range(3):
            for x in range(4):
                t = x * 32 + col * 3 + c
                fill_low.append(pltpu.roll(izr[0], lax.rem(128 - t, 128), 1))
                fill_high.append(pltpu.roll(izr[1], 127 - t, 1))
        lane = iota(u.shape, 3)
        near = near + jnp.where(lane == 0, jnp.stack(fill_low).reshape(u.shape), pltpu.roll(u, 1, 3))
        near = near + jnp.where(lane == 127, jnp.stack(fill_high).reshape(u.shape), pltpu.roll(u, 127, 3))
        total = (u[0] + u[1] + u[2])[None]
        r = ld[pl.ds(start, 96), :].reshape(3, 4, 8, 128)
        r = r - diag_own[None] * u + stiff_own[None] * (near - COUPLING * total)
        res[pl.ds(start, 96), :] = r.reshape(96, 128)
        return carry

    lax.fori_loop(0, 8, own_residual, 0)

    def pack_rows(f, carry):
        for side in range(2):
            for layer in range(2):
                ys[side, f, layer * 4 : layer * 4 + 4] = res[pl.ds(f * 32 + side * 6 + layer, 4, stride=8), :]
        return carry

    lax.fori_loop(0, FIELDS, pack_rows, 0, unroll=2)
    res_y = {}

    def send_rows(ch):
        fs = pl.ds(ch * PER, PER)
        res_y[ch] = exchange("gy", ys.at[0, fs], yr.at[1, fs], ys.at[1, fs], yr.at[0, fs])

    send_rows(0)
    send_rows(1)

    local[3].wait()

    def prepare_basis(k, carry):
        for cx in range(12):
            v = jnp.concatenate([bas[pl.ds((k * 4 + i) * 96 + cx * 8, 8), :] for i in range(4)], 0)
            rows = pl.ds(pl.multiple_of(k * 32, 32), 32)
            bh[rows, cx * 128 : cx * 128 + 128], bl[rows, cx * 128 : cx * 128 + 128] = halves(v)
        return carry

    lax.fori_loop(0, 8, prepare_basis, 0)
    for side in range(2):
        for cx in range(12):
            at = slice((side * 12 + cx) * 128, (side * 12 + cx) * 128 + 128)
            bf[0:32, at], bf[32:64, at] = halves(bas[pl.ds(cx * 8 + side * 7, 32, stride=96), :])

    def two(v):
        hi, lo = halves(v)
        return jnp.concatenate([hi, lo], 0)

    def coefficients(k, total):
        v = jnp.concatenate(
            [
                jnp.concatenate([res[pl.ds(col * 96 + (k * 2 + i) * 8, 8), :] for col in range(8)], 0)
                for i in range(2)
            ],
            1,
        )
        at = pl.ds(pl.multiple_of(k * 256, 256), 256)
        hi, lo = halves(v)
        total = total + lax.dot_general(hi, bh[:, at], NT, preferred_element_type=F32)
        total = total + lax.dot_general(lo, bh[:, at], NT, preferred_element_type=F32)
        return total + lax.dot_general(hi, bl[:, at], NT, preferred_element_type=F32)

    pairs = lax.fori_loop(0, 6, coefficients, jnp.zeros((64, 256), F32), unroll=6)
    equal = iota((64, 256), 0) % 8 == iota((64, 256), 1) % 8
    sums = jnp.sum(jnp.where(equal, pairs, 0.0).reshape(8, 8, 256), 1)
    fold = (iota((256, 128), 0) // 8 == iota((256, 128), 1)).astype(BF16)
    folded = jnp.dot(two(sums), fold, preferred_element_type=F32)
    coeff = folded[0:8] + folded[8:16]
    unfold = (iota((128, 256), 0) == iota((128, 256), 1) // 8).astype(BF16)

    local[4].wait()

    def prepare_coarse(k, carry):
        at = pl.ds(pl.multiple_of(k * 512, 512), 512)
        hi, lo = halves(ci[:, at])
        c2[0:32, at] = hi
        c2[32:64, at] = lo
        return carry

    lax.fori_loop(0, ci.shape[1] // 512, prepare_coarse, 0, unroll=2)

    cls_y()
    cls_x = exchange("gx", cbox.at[:, 2:4], cbox.at[:, 6:8], cbox.at[:, 4:6], cbox.at[:, 0:2])
    cls_x()
    low = jnp.zeros((8, 128), I32)
    high = jnp.zeros((8, 128), I32)
    for y in range(12):
        mask = lane8 // 2 == y
        low = jnp.where(mask, pltpu.roll(cbox[y], 2 * y, 1), low)
        high = jnp.where(mask, pltpu.roll(cbox[y], 2 * y + 2, 1), high)
    czs[0] = low
    czs[1] = high
    cls_z = exchange("gz", czs.at[0], czr.at[1], czs.at[1], czr.at[0])
    cls_z()

    def z_lanes(low, high, t, width):
        odd = lane8 % 2 == 1
        low, high = pltpu.roll(low, (128 - t) % 128, 1), pltpu.roll(high, (128 - t) % 128, 1)
        inner = jnp.where(odd, low, high)
        outer = jnp.where(odd, pltpu.roll(low, 1, 1), pltpu.roll(high, 127, 1))
        zero = jnp.zeros_like(inner)
        return jnp.where(lane8 < width, inner, zero) + pltpu.roll(jnp.where(lane8 < width, outer, zero), 64, 1)

    def factors(shifted):
        inside = shifted > 0
        stiff = lookup(shifted - 1, stiffness)
        mass = lookup(shifted - 1, density)
        weight = jnp.where(inside, DAMPING / jnp.where(inside, 6.0 * stiff + mass - COUPLING * stiff, 1.0), 0.0)
        return stiff, weight

    def box_factors(y, carry):
        stiff, weight = factors(cbox[y])
        sbox[y] = stiff
        wbox[y] = weight
        bbox[y] = stiff * weight
        spread = z_lanes(czr[0], czr[1], 2 * y, 2)
        pair = spread + pltpu.roll(spread, 2, 1)
        spread = pair + pltpu.roll(pair, 4, 1) + pltpu.roll(pair, 8, 1)
        stiff, weight = factors(spread)
        zw[y] = weight
        zb[y] = stiff * weight
        return carry

    lax.fori_loop(0, 12, box_factors, 0, unroll=6)

    it_y()
    parts = []
    for side in range(2):
        row = cls[pl.ds(side * 7, 4, stride=8), :]
        stiff = lookup(jnp.concatenate([row, row], 0), stiffness)
        vy[side] = (iyr[side].reshape(12, 8, 128) * stiff[None]).reshape(96, 128)
    for side in range(2):
        for cx in range(12):
            parts.append(vy[side, pl.ds(cx, 8, stride=12), :])
    faces = lax.dot_general(two(jnp.concatenate(parts, 1)), bf[...], NT, preferred_element_type=F32)

    def quarters(v):
        v = v[0:8] + v[8:16]
        v = v[:, 0:32] + v[:, 32:64]
        return jnp.concatenate([v, jnp.zeros((8, 96), F32)], 1)

    mine = coeff + quarters(faces)
    packed = zero8
    for q in range(4):
        v = pltpu.roll(mine, 32 * q, 1) if q else mine
        v = pltpu.roll(v, 8 - q, 0) if q else v
        packed = jnp.where(lane8 // 32 == q, v, packed)
    g1[pz, 0:1] = packed[0:1]
    g1[pz, 1:2] = packed[4:5]
    line = count[0]
    count[0] += nz
    plane = count[0]
    count[0] += nx * ny
    twins = count[0]
    count[0] += nx * ny

    def along_line(k):
        to = chip(px, py, lax.rem(pz + k, nz), core)
        return pltpu.make_async_remote_copy(g1.at[pz], g1.at[pz], ss.at[line + k], rs.at[line + k], to, MESH)

    def start_line(k, carry):
        along_line(k).start()
        return carry

    lax.fori_loop(1, nz, start_line, 0)
    send_rows(2)
    send_rows(3)
    for side in range(2):
        at = pl.ds(side * 7, 96, stride=8)
        res[at, :] = res[at, :] + vy[side]

    def own_rows(f, carry):
        for y in range(8):
            box[f, y + 2, 2:6] = res[pl.ds(f * 32 + y, 4, stride=8), :]
        return carry

    lax.fori_loop(0, FIELDS, own_rows, 0, unroll=2)
    own_x = exchange("gx", box.at[:, 2:10, 2:4], box.at[:, 2:10, 6:8], box.at[:, 2:10, 4:6], box.at[:, 2:10, 0:2])

    res_x, res_z = {}, {}

    def rows_arrive(ch):
        res_y[ch]()
        fs = pl.ds(ch * PER, PER)
        _, has_lower, _, has_upper = steps["gy"]

        @pl.when(has_lower)
        def _():
            for f in range(ch * PER, ch * PER + PER):
                v = yr[0, f]
                box[f, 0, 2:6] = v[0:4]
                box[f, 1, 2:6] = v[4:8] + sbox[1, 2:6] * iys[0, f * 4 : f * 4 + 4]

        @pl.when(has_upper)
        def _():
            for f in range(ch * PER, ch * PER + PER):
                v = yr[1, f]
                box[f, 10, 2:6] = v[0:4] + sbox[10, 2:6] * iys[1, f * 4 : f * 4 + 4]
                box[f, 11, 2:6] = v[4:8]

        first = exchange("gx", box.at[fs, 0:2, 2:4], box.at[fs, 0:2, 6:8], box.at[fs, 0:2, 4:6], box.at[fs, 0:2, 0:2])
        second = exchange(
            "gx", box.at[fs, 10:12, 2:4], box.at[fs, 10:12, 6:8], box.at[fs, 10:12, 4:6], box.at[fs, 10:12, 0:2]
        )
        res_x[ch] = (first, second)

    def planes_arrive(ch):
        if ch == 0:
            own_x()
        for arrived in res_x[ch]:
            arrived()
        lane = iota((12, 8, 128), 2)
        low = jnp.zeros((12, 8, 128), F32)
        high = jnp.zeros((12, 8, 128), F32)
        for i in range(PER):
            v = box[ch * PER + i]
            mask = lane // 2 == i
            low = jnp.where(mask, pltpu.roll(v, 2 * i, 2) if i else v, low)
            high = jnp.where(mask, pltpu.roll(v, 2 * i + 2, 2), high)
        for side, v in enumerate((low, high)):
            first, second = zero8, zero8
            for y in range(12):
                t = (y % 10) * 12
                w = pltpu.roll(v[y], t, 1) if t else v[y]
                if y < 10:
                    first = first + w
                else:
                    second = second + w
            zs[ch, side, 0] = first
            zs[ch, side, 1] = second
        res_z[ch] = exchange("gz", zs.at[ch, 0], zr.at[ch, 1], zs.at[ch, 1], zr.at[ch, 0])

    def sweep(src, zsrc, dst, zdst, y):
        e, z = src[:, y], zsrc[y]
        lane, lane6 = lane8, iota((PER, 8, 128), 2)
        near = src[:, y - 1] + src[:, y + 1] + beside_x(e, 1)
        fill = jnp.stack([pltpu.roll(z, 127 - 2 * i, 1) for i in range(PER)])
        near = near + jnp.where(lane6 == 0, fill, pltpu.roll(e, 1, 2))
        near = near + jnp.where(lane6 == 127, fill, pltpu.roll(e, 127, 2))
        totals = jnp.stack([e[0] + e[1] + e[2]] * 3 + [e[3] + e[4] + e[5]] * 3)
        dst_value = ga[:, y] + (1.0 - DAMPING) * e + bbox[y - 1][None] * (near - COUPLING * totals)
        if zdst is not None:
            dst[:, y] = dst_value
            push = jnp.zeros((8, 128), F32)
            for i in range(PER):
                push = jnp.where(lane // 2 == i, pltpu.roll(e[i], 2 * i + 1, 1), push)
            znear = zsrc[y - 1] + zsrc[y + 1] + beside_x(z, 0) + push + pltpu.roll(z, 64, 1)
            two_on, four_on = pltpu.roll(z, 126, 1), pltpu.roll(z, 124, 1)
            two_back, four_back = pltpu.roll(z, 2, 1), pltpu.roll(z, 4, 1)
            comp = ((lane % 64) // 2) % 3
            rest = jnp.where(
                comp == 0, two_on + four_on, jnp.where(comp == 1, two_on + two_back, two_back + four_back)
            )
            zdst[y] = za[y] + (1.0 - DAMPING) * z + zb[y - 1] * (znear - COUPLING * (z + rest))
        return dst_value

    def sweeps(ch):
        res_z[ch]()

        def start(y, carry):
            ga[:, y + 1] = box[pl.ds(ch * PER, PER), y] * wbox[y][None]
            return carry

        lax.fori_loop(0, 12, start, 0)
        for y in range(12):
            t = (y % 10) * 12
            z = z_lanes(zr[ch, 0, y // 10], zr[ch, 1, y // 10], t, 2 * PER)
            za[y + 1] = z * zw[y]

        def first(y, carry):
            sweep(ga, za, gb, zc, y)
            return carry

        lax.fori_loop(1, 13, first, 0, unroll=12)

        def second(y, carry):
            sweep(gb, zc, gc, zd, y)
            return carry

        lax.fori_loop(2, 12, second, 0, unroll=10)

        def third(y, carry):
            v = sweep(gc, zd, None, None, y)
            for i in range(PER):
                at = pl.ds((ch * PER + i) * 32 + y - 3, 4, stride=8)
                acc[at, :] = acc[at, :] + v[i, 2:6]
            return carry

        lax.fori_loop(3, 11, third, 0, unroll=8)

    def block(x, y, c):
        return (y * 2 + c) * nx + x

    def along_plane(p):
        x, y = other(p, 1)
        b = block(px, py, core)
        return pltpu.make_async_remote_copy(
            g2.at[b], g2.at[b], ss.at[plane + p], rs.at[plane + p], chip(x, y, pz, core), MESH
        )

    def to_twin(p):
        x, y = other(p, -1)
        b = block(x, y, core)
        return pltpu.make_async_remote_copy(g2.at[b], g2.at[b], ss.at[twins + p], rs.at[twins + p], twin, MESH)

    def line_arrives():
        def arrive(k, carry):
            along_line(k).wait_recv()
            return carry

        lax.fori_loop(1, nz, arrive, 0)
        groups = nz // 4
        rows = g1[...]
        upper = jnp.broadcast_to(rows[:, 0:1], (nz, 8, 128))
        lower = jnp.broadcast_to(rows[:, 1:2], (nz, 8, 128))
        both = jnp.where(iota((nz, 8, 128), 1) < 4, upper, lower).reshape(groups, 4, 8, 128)
        lane, sub = iota((groups, 8, 128), 2) // 32, iota((groups, 8, 128), 1) % 4
        spread = jnp.zeros((groups, 8, 128), F32)
        for zz in range(4):
            for q in range(4):
                t = 32 * ((zz - q) % 4)
                v = both[:, zz]
                v = pltpu.roll(v, t, 2) if t else v
                spread = jnp.where((lane == zz) & (sub == q), v, spread)
        b = block(px, py, core)
        g2[b] = jnp.concatenate([spread[i] for i in range(groups)], 1)

        def start(p, carry):
            along_plane(p).start()
            return carry

        lax.fori_loop(1, nx * ny, start, 0)
        to_twin(0).start()

    width = nz * 32

    def times_block(b, total):
        at = pl.ds(pl.multiple_of(b * width, width), width)
        return total + lax.dot_general(two(g2[b]), c2[:, at], NT, preferred_element_type=F32)

    def plane_arrives():
        def arrive(p, total):
            along_plane(p).wait_recv()
            to_twin(p).start()
            x, y = other(p, -1)
            return times_block(block(x, y, core), total)

        return lax.fori_loop(1, nx * ny, arrive, times_block(block(px, py, core), jnp.zeros((16, 64), F32)))

    def twins_arrive(total):
        def arrive(p, total):
            to_twin(p).wait_recv()
            x, y = other(p, -1)
            return times_block(block(x, y, 1 - core), total)

        total = lax.fori_loop(0, nx * ny, arrive, total)
        solved = quarters(total)
        spread = jnp.dot(two(solved), unfold, preferred_element_type=F32)
        spread = spread[0:8] + spread[8:16]
        rows = jnp.broadcast_to(spread[:, None], (8, 8, 256)).reshape(64, 256)
        hi, lo = halves(jnp.where(equal, rows, 0.0))

        def correct(k, carry):
            at = pl.ds(pl.multiple_of(k * 256, 256), 256)
            v = jnp.dot(hi, bh[:, at], preferred_element_type=F32)
            v = v + jnp.dot(lo, bh[:, at], preferred_element_type=F32)
            v = v + jnp.dot(hi, bl[:, at], preferred_element_type=F32)
            for col in range(8):
                for i in range(2):
                    rows = pl.ds(pl.multiple_of(col * 96 + (k * 2 + i) * 8, 8), 8)
                    acc[rows, :] = acc[rows, :] + v[col * 8 : col * 8 + 8, i * 128 : i * 128 + 128]
            return carry

        lax.fori_loop(0, 6, correct, 0, unroll=6)

    rows_arrive(0)
    rows_arrive(1)
    planes_arrive(0)
    line_arrives()
    planes_arrive(1)
    sweeps(0)
    rows_arrive(2)
    sweeps(1)
    planes_arrive(2)
    rows_arrive(3)
    total = plane_arrives()
    twins_arrive(total)
    sweeps(2)
    planes_arrive(3)
    sweeps(3)

    for sent in pending:
        sent()

    def all_sent(k, carry):
        along_line(k).wait_send()
        return carry

    lax.fori_loop(1, nz, all_sent, 0)

    def all_sent_plane(p, carry):
        along_plane(p).wait_send()
        to_twin(p).wait_send()
        return carry

    to_twin(0).wait_send()
    lax.fori_loop(1, nx * ny, all_sent_plane, 0)


def solution(mesh):
    ny, nx, nz = mesh.shape["gx"] // 2, mesh.shape["gy"] // 2, mesh.shape["gz"] * 2
    nc = 2 * ny * nx * nz * 32

    def step(loads, iterate, classes, stiffness, density, basis, coarse_inverse):
        v = pltpu.VMEM
        scratch = [
            v((768, 128), F32), v((768, 128), F32), v((32, 128), I32),
            pltpu.SMEM((8,), F32), pltpu.SMEM((8,), F32), v((3072, 128), F32),
            v((32, nc), F32), v((768, 128), F32),
            v((2, 96, 128), F32), v((2, 96, 128), F32), v((2, FIELDS, 8, 128), F32), v((2, FIELDS, 8, 128), F32),
            v((2, 8, 128), F32), v((2, 8, 128), F32),
            v((12, 8, 128), I32), v((2, 8, 128), I32), v((2, 8, 128), I32),
            v((FIELDS, 12, 8, 128), F32), v((2, FIELDS, 8, 128), F32), v((2, FIELDS, 8, 128), F32),
            v((CHUNKS, 2, 2, 8, 128), F32), v((CHUNKS, 2, 2, 8, 128), F32),
            v((256, 1536), BF16), v((256, 1536), BF16), v((64, 3072), BF16), v((64, nc), BF16),
            v((nz, 2, 128), F32), v((2 * ny * nx, 8, nz * 32), F32),
            v((12, 8, 128), F32), v((12, 8, 128), F32), v((12, 8, 128), F32), v((12, 8, 128), F32),
            v((12, 8, 128), F32),
            v((PER, 14, 8, 128), F32), v((PER, 14, 8, 128), F32), v((PER, 14, 8, 128), F32),
            v((14, 8, 128), F32), v((14, 8, 128), F32), v((14, 8, 128), F32),
            v((2, 96, 128), F32),
            pltpu.SemaphoreType.DMA((128,)), pltpu.SemaphoreType.DMA((128,)), pltpu.SemaphoreType.DMA((7,)),
        ]
        hbm = pl.BlockSpec(memory_space=pltpu.HBM)
        result = pl.pallas_call(
            functools.partial(kernel, ny, nx, nz),
            out_shape=jax.ShapeDtypeStruct((768, 128), F32),
            in_specs=[hbm] * 7,
            out_specs=pl.BlockSpec(memory_space=pltpu.VMEM),
            scratch_shapes=scratch,
            compiler_params=pltpu.CompilerParams(
                collective_id=0, has_side_effects=True, vmem_limit_bytes=64 * 1024 * 1024
            ),
            name="schwarz",
        )(
            loads.reshape(768, 128), iterate.reshape(768, 128), classes.reshape(32, 128), stiffness, density,
            basis.reshape(3072, 128), coarse_inverse,
        )
        return result.reshape(iterate.shape)

    field = P(None, None, "gx", "gy", "gz")
    return jax.shard_map(
        step,
        mesh=mesh,
        in_specs=(field, field, P("gx", "gy", "gz"), P(), P(), field, P(("gx", "gy", "gz"), None)),
        out_specs=field,
        check_vma=False,
    )
```

```python
import functools

import jax
import jax.numpy as jnp
from jax import lax
from jax.experimental import pallas as pl
from jax.experimental.pallas import tpu as pltpu
from jax.sharding import PartitionSpec as P

MESH = pl.DeviceIdType.MESH
F32, BF16, I32 = jnp.float32, jnp.bfloat16, jnp.int32
FIELDS = 24
CHUNKS, PER = 4, 6
COUPLING, DAMPING = 0.1, 0.7
NT = (((1,), (1,)), ((), ()))


def lookup(classes, table):
    found = jnp.zeros(classes.shape, F32)
    for k in range(8):
        found = found + jnp.where(classes == k, table[k], 0.0)
    return found


def halves(v):
    high = v.astype(BF16)
    return high, (v - high.astype(F32)).astype(BF16)


def iota(shape, axis):
    return lax.broadcasted_iota(I32, shape, axis)


def beside_x(v, axis):
    row = iota(v.shape, axis)
    return jnp.where(row == 0, 0.0, pltpu.roll(v, 1, axis)) + jnp.where(row == 7, 0.0, pltpu.roll(v, 7, axis))


def kernel(
    ny, nx, nz, loads, iterate, classes, stiffness_in, density_in, basis, cinv, acc,
    it, ld, cls, stiffness, density, bas, ci, res, iys, iyr, ixs, ixr, izs, izr, cbox, czs, czr, box, ys, yr,
    zs, zr, bh, bl, bf, wide, c2, g1, g2, sbox, wbox, bbox, zw, zb, ga, gb, gc, za, zc, zd, vy,
    ss, rs, ls,
):
    gx, gy, gz = lax.axis_index("gx"), lax.axis_index("gy"), lax.axis_index("gz")
    half = nz // 2
    py, core, px, pz = gx // 2, gx % 2, gy // 2, (gy % 2) * half + gz

    def chip(x, y, z, c):
        return (y * 2 + c, x * 2 + z // half, z % half)

    steps = {
        "gx": ((gx - 1, gy, gz), gx > 0, (gx + 1, gy, gz), gx < 2 * ny - 1),
        "gy": ((gx, gy - 1, gz), gy > 0, (gx, gy + 1, gz), gy < 2 * nx - 1),
        "gz": ((gx, gy, gz - 1), gz > 0, (gx, gy, gz + 1), gz < half - 1),
    }
    count = [0]
    pending = []

    def exchange(axis, low_src, low_dst, high_src, high_dst):
        lower, has_lower, upper, has_upper = steps[axis]
        i = count[0]
        count[0] += 2
        down = pltpu.make_async_remote_copy(low_src, low_dst, ss.at[i], rs.at[i], lower, MESH)
        up = pltpu.make_async_remote_copy(high_src, high_dst, ss.at[i + 1], rs.at[i + 1], upper, MESH)
        pl.when(has_lower)(down.start)
        pl.when(has_upper)(up.start)

        def sent():
            pl.when(has_lower)(down.wait_send)
            pl.when(has_upper)(up.wait_send)

        def arrived():
            pl.when(has_upper)(down.wait_recv)
            pl.when(has_lower)(up.wait_recv)

        pending.append(sent)
        return arrived

    local = [
        pltpu.make_async_copy(a, b, ls.at[i])
        for i, (a, b) in enumerate(
            (
                (iterate, it), (classes, cls), (loads, ld), (basis, bas), (cinv, ci),
                (stiffness_in, stiffness), (density_in, density),
            )
        )
    ]
    for copy in local:
        copy.start()

    for ref in (iyr, ixr, izr, cbox, czr, box, yr, zr):
        ref[...] = jnp.zeros(ref.shape, ref.dtype)

    barrier = pltpu.get_barrier_semaphore()
    high_half = gy % 2
    across_gx = jnp.where(core == 1, gx < 2 * ny - 1, gx > 0)
    across_gy = jnp.where(high_half == 1, gy < 2 * nx - 1, gy > 0)
    for there, to in ((across_gx, (gx + 2 * core - 1, gy, gz)), (across_gy, (gx, gy + 2 * high_half - 1, gz))):
        pl.when(there)(functools.partial(pl.semaphore_signal, barrier, inc=1, device_id=to, device_id_type=MESH))

    def greet_line(k, carry):
        pl.semaphore_signal(barrier, inc=1, device_id=chip(px, py, lax.rem(pz + k, nz), core), device_id_type=MESH)
        return carry

    lax.fori_loop(1, nz, greet_line, 0)

    def other(p, sign):
        dx, dy = p // ny, lax.rem(p, ny)
        return lax.rem(px + sign * dx + nx, nx), lax.rem(py + sign * dy + ny, ny)

    def greet_plane(p, carry):
        x, y = other(p, 1)
        pl.semaphore_signal(barrier, inc=1, device_id=chip(x, y, pz, core), device_id_type=MESH)
        return carry

    lax.fori_loop(1, nx * ny, greet_plane, 0)
    twin = chip(px, py, pz, 1 - core)
    pl.semaphore_signal(barrier, inc=1, device_id=twin, device_id_type=MESH)

    lane8 = iota((8, 128), 1)
    sub8 = iota((8, 128), 0)

    local[0].wait()
    iys[0] = it[pl.ds(0, 96, stride=8), :]
    iys[1] = it[pl.ds(7, 96, stride=8), :]

    def pack_iterate(f, carry):
        low, high = carry
        start = pl.multiple_of(f * 32, 32)
        ixs[0, f] = it[pl.ds(start, 8), :]
        ixs[1, f] = it[pl.ds(start + 24, 8), :]
        for x in range(4):
            v = it[pl.ds(start + x * 8, 8), :]
            t = x * 32 + f
            low = jnp.where(lane8 == t, pltpu.roll(v, t, 1), low)
            high = jnp.where(lane8 == t, pltpu.roll(v, t + 1, 1), high)
        return low, high

    zero8 = jnp.zeros((8, 128), F32)
    low, high = lax.fori_loop(0, FIELDS, pack_iterate, (zero8, zero8), unroll=2)
    izs[0] = low
    izs[1] = high
    local[1].wait()
    for y in range(8):
        cbox[y + 2, 2:6] = cls[pl.ds(y, 4, stride=8), :] + 1

    acc[...] = it[...]
    for ref in (ga, gb, gc):
        ref[:, 0] = jnp.zeros((PER, 8, 128), F32)
        ref[:, 13] = jnp.zeros((PER, 8, 128), F32)
    for ref in (za, zc, zd):
        ref[0] = zero8
        ref[13] = zero8

    peers = nz - 1 + nx * ny - 1 + 1 + across_gx.astype(I32) + across_gy.astype(I32)
    pl.semaphore_wait(barrier, peers)

    it_y = exchange("gy", iys.at[0], iyr.at[1], iys.at[1], iyr.at[0])
    cls_y = exchange("gy", cbox.at[2:4, 2:6], cbox.at[10:12, 2:6], cbox.at[8:10, 2:6], cbox.at[0:2, 2:6])
    it_x = exchange("gx", ixs.at[0], ixr.at[1], ixs.at[1], ixr.at[0])
    it_z = exchange("gz", izs.at[0], izr.at[1], izs.at[1], izr.at[0])

    local[5].wait()
    local[6].wait()
    local[2].wait()

    def own_class(x):
        return cls[pl.ds(x * 8, 8), :]

    stiff_own = jnp.stack([lookup(own_class(x), stiffness) for x in range(4)])
    mass_own = jnp.stack([lookup(own_class(x), density) for x in range(4)])
    diag_own = 6.0 * stiff_own + mass_own - COUPLING * stiff_own

    it_x()
    it_z()

    def own_residual(col, carry):
        start = pl.multiple_of(col * 96, 96)
        u = it[pl.ds(start, 96), :].reshape(3, 4, 8, 128)
        lower = ixr[0, pl.ds(col * 3, 3)][:, None]
        upper = ixr[1, pl.ds(col * 3, 3)][:, None]
        near = jnp.concatenate([lower, u[:, :3]], 1) + jnp.concatenate([u[:, 1:], upper], 1)
        near = near + beside_x(u, 2)
        fill_low, fill_high = [], []
        for c in range(3):
            for x in range(4):
                t = x * 32 + col * 3 + c
                fill_low.append(pltpu.roll(izr[0], lax.rem(128 - t, 128), 1))
                fill_high.append(pltpu.roll(izr[1], 127 - t, 1))
        lane = iota(u.shape, 3)
        near = near + jnp.where(lane == 0, jnp.stack(fill_low).reshape(u.shape), pltpu.roll(u, 1, 3))
        near = near + jnp.where(lane == 127, jnp.stack(fill_high).reshape(u.shape), pltpu.roll(u, 127, 3))
        total = (u[0] + u[1] + u[2])[None]
        r = ld[pl.ds(start, 96), :].reshape(3, 4, 8, 128)
        r = r - diag_own[None] * u + stiff_own[None] * (near - COUPLING * total)
        res[pl.ds(start, 96), :] = r.reshape(96, 128)
        return carry

    lax.fori_loop(0, 8, own_residual, 0)

    def pack_rows(f, carry):
        for side in range(2):
            for layer in range(2):
                ys[side, f, layer * 4 : layer * 4 + 4] = res[pl.ds(f * 32 + side * 6 + layer, 4, stride=8), :]
        return carry

    lax.fori_loop(0, FIELDS, pack_rows, 0, unroll=2)
    res_y = {}

    def send_rows(ch):
        fs = pl.ds(ch * PER, PER)
        res_y[ch] = exchange("gy", ys.at[0, fs], yr.at[1, fs], ys.at[1, fs], yr.at[0, fs])

    send_rows(0)
    send_rows(1)
    send_rows(2)

    local[3].wait()

    def prepare_basis(k, carry):
        for cx in range(12):
            v = jnp.concatenate([bas[pl.ds((k * 4 + i) * 96 + cx * 8, 8), :] for i in range(4)], 0)
            rows = pl.ds(pl.multiple_of(k * 32, 32), 32)
            bh[rows, cx * 128 : cx * 128 + 128], bl[rows, cx * 128 : cx * 128 + 128] = halves(v)
        return carry

    lax.fori_loop(0, 8, prepare_basis, 0)
    for side in range(2):
        for cx in range(12):
            at = slice((side * 12 + cx) * 128, (side * 12 + cx) * 128 + 128)
            bf[0:32, at], bf[32:64, at] = halves(bas[pl.ds(cx * 8 + side * 7, 32, stride=96), :])

    def two(v):
        hi, lo = halves(v)
        return jnp.concatenate([hi, lo], 0)

    def coefficients(k, total):
        v = jnp.concatenate(
            [
                jnp.concatenate([res[pl.ds(col * 96 + (k * 2 + i) * 8, 8), :] for col in range(8)], 0)
                for i in range(2)
            ],
            1,
        )
        at = pl.ds(pl.multiple_of(k * 256, 256), 256)
        hi, lo = halves(v)
        total = total + lax.dot_general(hi, bh[:, at], NT, preferred_element_type=F32)
        total = total + lax.dot_general(lo, bh[:, at], NT, preferred_element_type=F32)
        return total + lax.dot_general(hi, bl[:, at], NT, preferred_element_type=F32)

    pairs = lax.fori_loop(0, 6, coefficients, jnp.zeros((64, 256), F32), unroll=6)
    equal = iota((64, 256), 0) % 8 == iota((64, 256), 1) % 8
    sums = jnp.sum(jnp.where(equal, pairs, 0.0).reshape(8, 8, 256), 1)
    fold = (iota((256, 128), 0) // 8 == iota((256, 128), 1)).astype(BF16)
    folded = jnp.dot(two(sums), fold, preferred_element_type=F32)
    coeff = folded[0:8] + folded[8:16]

    local[4].wait()

    def prepare_coarse(k, carry):
        at = pl.ds(pl.multiple_of(k * 512, 512), 512)
        hi, lo = halves(ci[:, at])
        c2[0:32, at] = hi
        c2[32:64, at] = lo
        return carry

    lax.fori_loop(0, ci.shape[1] // 512, prepare_coarse, 0, unroll=2)

    cls_y()
    cls_x = exchange("gx", cbox.at[:, 2:4], cbox.at[:, 6:8], cbox.at[:, 4:6], cbox.at[:, 0:2])

    it_y()
    parts = []
    for side in range(2):
        row = cls[pl.ds(side * 7, 4, stride=8), :]
        stiff = lookup(jnp.concatenate([row, row], 0), stiffness)
        vy[side] = (iyr[side].reshape(12, 8, 128) * stiff[None]).reshape(96, 128)
    for side in range(2):
        for cx in range(12):
            parts.append(vy[side, pl.ds(cx, 8, stride=12), :])
    faces = lax.dot_general(two(jnp.concatenate(parts, 1)), bf[...], NT, preferred_element_type=F32)

    def quarters(v):
        v = v[0:8] + v[8:16]
        v = v[:, 0:32] + v[:, 32:64]
        return jnp.concatenate([v, jnp.zeros((8, 96), F32)], 1)

    mine = coeff + quarters(faces)
    packed = zero8
    for q in range(4):
        v = pltpu.roll(mine, 32 * q, 1) if q else mine
        v = pltpu.roll(v, 8 - q, 0) if q else v
        packed = jnp.where(lane8 // 32 == q, v, packed)
    g1[pz, 0:1] = packed[0:1]
    g1[pz, 1:2] = packed[4:5]
    line = count[0]
    count[0] += nz
    plane = count[0]
    count[0] += nx * ny
    twins = count[0]
    count[0] += nx * ny

    def along_line(k):
        to = chip(px, py, lax.rem(pz + k, nz), core)
        return pltpu.make_async_remote_copy(g1.at[pz], g1.at[pz], ss.at[line + k], rs.at[line + k], to, MESH)

    def start_line(k, carry):
        along_line(k).start()
        return carry

    lax.fori_loop(1, nz, start_line, 0)
    send_rows(3)
    for side in range(2):
        at = pl.ds(side * 7, 96, stride=8)
        res[at, :] = res[at, :] + vy[side]

    cls_x()
    low = jnp.zeros((8, 128), I32)
    high = jnp.zeros((8, 128), I32)
    for y in range(12):
        mask = lane8 // 2 == y
        low = jnp.where(mask, pltpu.roll(cbox[y], 2 * y, 1), low)
        high = jnp.where(mask, pltpu.roll(cbox[y], 2 * y + 2, 1), high)
    czs[0] = low
    czs[1] = high
    cls_z = exchange("gz", czs.at[0], czr.at[1], czs.at[1], czr.at[0])

    def own_rows(f, carry):
        for y in range(8):
            box[f, y + 2, 2:6] = res[pl.ds(f * 32 + y, 4, stride=8), :]
        return carry

    lax.fori_loop(0, FIELDS, own_rows, 0, unroll=2)
    own_x = exchange("gx", box.at[:, 2:10, 2:4], box.at[:, 2:10, 6:8], box.at[:, 2:10, 4:6], box.at[:, 2:10, 0:2])


    def z_lanes(low, high, t, width):
        odd = lane8 % 2 == 1
        low, high = pltpu.roll(low, (128 - t) % 128, 1), pltpu.roll(high, (128 - t) % 128, 1)
        inner = jnp.where(odd, low, high)
        outer = jnp.where(odd, pltpu.roll(low, 1, 1), pltpu.roll(high, 127, 1))
        zero = jnp.zeros_like(inner)
        return jnp.where(lane8 < width, inner, zero) + pltpu.roll(jnp.where(lane8 < width, outer, zero), 64, 1)

    cls_z()

    def factors(shifted):
        inside = shifted > 0
        stiff = lookup(shifted - 1, stiffness)
        mass = lookup(shifted - 1, density)
        weight = jnp.where(inside, DAMPING / jnp.where(inside, 6.0 * stiff + mass - COUPLING * stiff, 1.0), 0.0)
        return stiff, weight

    def box_factors(y, carry):
        stiff, weight = factors(cbox[y])
        sbox[y] = stiff
        wbox[y] = weight
        bbox[y] = stiff * weight
        spread = z_lanes(czr[0], czr[1], 2 * y, 2)
        pair = spread + pltpu.roll(spread, 2, 1)
        spread = pair + pltpu.roll(pair, 4, 1) + pltpu.roll(pair, 8, 1)
        stiff, weight = factors(spread)
        zw[y] = weight
        zb[y] = stiff * weight
        return carry

    lax.fori_loop(0, 12, box_factors, 0, unroll=6)

    res_x, res_z = {}, {}

    def rows_arrive(ch):
        res_y[ch]()
        fs = pl.ds(ch * PER, PER)
        _, has_lower, _, has_upper = steps["gy"]

        @pl.when(has_lower)
        def _():
            for f in range(ch * PER, ch * PER + PER):
                v = yr[0, f]
                box[f, 0, 2:6] = v[0:4]
                box[f, 1, 2:6] = v[4:8] + sbox[1, 2:6] * iys[0, f * 4 : f * 4 + 4]

        @pl.when(has_upper)
        def _():
            for f in range(ch * PER, ch * PER + PER):
                v = yr[1, f]
                box[f, 10, 2:6] = v[0:4] + sbox[10, 2:6] * iys[1, f * 4 : f * 4 + 4]
                box[f, 11, 2:6] = v[4:8]

        first = exchange("gx", box.at[fs, 0:2, 2:4], box.at[fs, 0:2, 6:8], box.at[fs, 0:2, 4:6], box.at[fs, 0:2, 0:2])
        second = exchange(
            "gx", box.at[fs, 10:12, 2:4], box.at[fs, 10:12, 6:8], box.at[fs, 10:12, 4:6], box.at[fs, 10:12, 0:2]
        )
        res_x[ch] = (first, second)

    def planes_arrive(ch):
        if ch == 0:
            own_x()
        for arrived in res_x[ch]:
            arrived()
        lane = iota((12, 8, 128), 2)
        low = jnp.zeros((12, 8, 128), F32)
        high = jnp.zeros((12, 8, 128), F32)
        for i in range(PER):
            v = box[ch * PER + i]
            mask = lane // 2 == i
            low = jnp.where(mask, pltpu.roll(v, 2 * i, 2) if i else v, low)
            high = jnp.where(mask, pltpu.roll(v, 2 * i + 2, 2), high)
        for side, v in enumerate((low, high)):
            first, second = zero8, zero8
            for y in range(12):
                t = (y % 10) * 12
                w = pltpu.roll(v[y], t, 1) if t else v[y]
                if y < 10:
                    first = first + w
                else:
                    second = second + w
            zs[ch, side, 0] = first
            zs[ch, side, 1] = second
        res_z[ch] = exchange("gz", zs.at[ch, 0], zr.at[ch, 1], zs.at[ch, 1], zr.at[ch, 0])

    def sweep(src, zsrc, dst, zdst, y):
        e, z = src[:, y], zsrc[y]
        lane, lane6 = lane8, iota((PER, 8, 128), 2)
        near = src[:, y - 1] + src[:, y + 1] + beside_x(e, 1)
        fill = jnp.stack([pltpu.roll(z, 127 - 2 * i, 1) for i in range(PER)])
        near = near + jnp.where(lane6 == 0, fill, pltpu.roll(e, 1, 2))
        near = near + jnp.where(lane6 == 127, fill, pltpu.roll(e, 127, 2))
        totals = jnp.stack([e[0] + e[1] + e[2]] * 3 + [e[3] + e[4] + e[5]] * 3)
        dst_value = ga[:, y] + (1.0 - DAMPING) * e + bbox[y - 1][None] * (near - COUPLING * totals)
        if zdst is not None:
            dst[:, y] = dst_value
            push = jnp.zeros((8, 128), F32)
            for i in range(PER):
                push = jnp.where(lane // 2 == i, pltpu.roll(e[i], 2 * i + 1, 1), push)
            znear = zsrc[y - 1] + zsrc[y + 1] + beside_x(z, 0) + push + pltpu.roll(z, 64, 1)
            two_on, four_on = pltpu.roll(z, 126, 1), pltpu.roll(z, 124, 1)
            two_back, four_back = pltpu.roll(z, 2, 1), pltpu.roll(z, 4, 1)
            comp = ((lane % 64) // 2) % 3
            rest = jnp.where(
                comp == 0, two_on + four_on, jnp.where(comp == 1, two_on + two_back, two_back + four_back)
            )
            zdst[y] = za[y] + (1.0 - DAMPING) * z + zb[y - 1] * (znear - COUPLING * (z + rest))
        return dst_value

    def sweeps(ch):
        res_z[ch]()

        def start(y, carry):
            ga[:, y + 1] = box[pl.ds(ch * PER, PER), y] * wbox[y][None]
            return carry

        lax.fori_loop(0, 12, start, 0)
        for y in range(12):
            t = (y % 10) * 12
            z = z_lanes(zr[ch, 0, y // 10], zr[ch, 1, y // 10], t, 2 * PER)
            za[y + 1] = z * zw[y]

        def first(y, carry):
            sweep(ga, za, gb, zc, y)
            return carry

        lax.fori_loop(1, 13, first, 0, unroll=12)

        def second(y, carry):
            sweep(gb, zc, gc, zd, y)
            return carry

        lax.fori_loop(2, 12, second, 0, unroll=10)

        def third(y, carry):
            v = sweep(gc, zd, None, None, y)
            for i in range(PER):
                at = pl.ds((ch * PER + i) * 32 + y - 3, 4, stride=8)
                acc[at, :] = acc[at, :] + v[i, 2:6]
            return carry

        lax.fori_loop(3, 11, third, 0, unroll=8)

    def block(x, y, c):
        return (y * 2 + c) * nx + x

    def along_plane(p):
        x, y = other(p, 1)
        b = block(px, py, core)
        return pltpu.make_async_remote_copy(
            g2.at[b], g2.at[b], ss.at[plane + p], rs.at[plane + p], chip(x, y, pz, core), MESH
        )

    def to_twin(p):
        x, y = other(p, -1)
        b = block(x, y, core)
        return pltpu.make_async_remote_copy(g2.at[b], g2.at[b], ss.at[twins + p], rs.at[twins + p], twin, MESH)

    def line_arrives():
        def arrive(k, carry):
            along_line(k).wait_recv()
            return carry

        lax.fori_loop(1, nz, arrive, 0)
        groups = nz // 4
        rows = g1[...]
        upper = jnp.broadcast_to(rows[:, 0:1], (nz, 8, 128))
        lower = jnp.broadcast_to(rows[:, 1:2], (nz, 8, 128))
        both = jnp.where(iota((nz, 8, 128), 1) < 4, upper, lower).reshape(groups, 4, 8, 128)
        lane, sub = iota((groups, 8, 128), 2) // 32, iota((groups, 8, 128), 1) % 4
        spread = jnp.zeros((groups, 8, 128), F32)
        for zz in range(4):
            for q in range(4):
                t = 32 * ((zz - q) % 4)
                v = both[:, zz]
                v = pltpu.roll(v, t, 2) if t else v
                spread = jnp.where((lane == zz) & (sub == q), v, spread)
        b = block(px, py, core)
        g2[b] = jnp.concatenate([spread[i] for i in range(groups)], 1)

        def start(p, carry):
            along_plane(p).start()
            return carry

        lax.fori_loop(1, nx * ny, start, 0)
        to_twin(0).start()

    width = nz * 32

    def times_blocks(c, total):
        def add(p, total):
            x, y = other(p, -1)
            b = block(x, y, c)
            at = pl.ds(pl.multiple_of(b * width, width), width)
            return total + lax.dot_general(two(g2[b]), c2[:, at], NT, preferred_element_type=F32)

        return lax.fori_loop(0, nx * ny, add, total, unroll=nx * ny)

    def plane_arrives():
        def arrive(p, carry):
            along_plane(p).wait_recv()
            to_twin(p).start()
            return carry

        lax.fori_loop(1, nx * ny, arrive, 0)
        return times_blocks(core, jnp.zeros((16, 64), F32))

    def twins_arrive(total):
        def arrive(p, carry):
            to_twin(p).wait_recv()
            return carry

        lax.fori_loop(0, nx * ny, arrive, 0)
        total = times_blocks(1 - core, total)
        solved = quarters(total)
        for j in range(32):
            column = jnp.broadcast_to(solved[:, j : j + 1], (8, 128))
            wide[j] = jnp.broadcast_to(column[:, None], (8, 8, 128))

        def correct(k, carry):
            def add(j, sums):
                parts = [bas[pl.ds(pl.multiple_of(j * 96 + k * 16 + i * 8, 8), 8), :] for i in range(2)]
                out = []
                for col in range(8):
                    factor = wide[j, col]
                    out += [sums[2 * col + i] + factor * parts[i] for i in range(2)]
                return tuple(out)

            sums = lax.fori_loop(0, 32, add, (zero8,) * 16, unroll=8)
            for col in range(8):
                for i in range(2):
                    rows = pl.ds(pl.multiple_of(col * 96 + k * 16 + i * 8, 8), 8)
                    acc[rows, :] = acc[rows, :] + sums[2 * col + i]
            return carry

        lax.fori_loop(0, 6, correct, 0)

    rows_arrive(0)
    rows_arrive(1)
    line_arrives()
    rows_arrive(2)
    rows_arrive(3)
    planes_arrive(0)
    planes_arrive(1)
    planes_arrive(2)
    planes_arrive(3)
    sweeps(0)
    total = plane_arrives()
    sweeps(1)
    sweeps(2)
    sweeps(3)
    twins_arrive(total)

    for sent in pending:
        sent()

    def all_sent(k, carry):
        along_line(k).wait_send()
        return carry

    lax.fori_loop(1, nz, all_sent, 0)

    def all_sent_plane(p, carry):
        along_plane(p).wait_send()
        to_twin(p).wait_send()
        return carry

    to_twin(0).wait_send()
    lax.fori_loop(1, nx * ny, all_sent_plane, 0)


def solution(mesh):
    ny, nx, nz = mesh.shape["gx"] // 2, mesh.shape["gy"] // 2, mesh.shape["gz"] * 2
    nc = 2 * ny * nx * nz * 32

    def step(loads, iterate, classes, stiffness, density, basis, coarse_inverse):
        v = pltpu.VMEM
        scratch = [
            v((768, 128), F32), v((768, 128), F32), v((32, 128), I32),
            pltpu.SMEM((8,), F32), pltpu.SMEM((8,), F32), v((3072, 128), F32),
            v((32, nc), F32), v((768, 128), F32),
            v((2, 96, 128), F32), v((2, 96, 128), F32), v((2, FIELDS, 8, 128), F32), v((2, FIELDS, 8, 128), F32),
            v((2, 8, 128), F32), v((2, 8, 128), F32),
            v((12, 8, 128), I32), v((2, 8, 128), I32), v((2, 8, 128), I32),
            v((FIELDS, 12, 8, 128), F32), v((2, FIELDS, 8, 128), F32), v((2, FIELDS, 8, 128), F32),
            v((CHUNKS, 2, 2, 8, 128), F32), v((CHUNKS, 2, 2, 8, 128), F32),
            v((256, 1536), BF16), v((256, 1536), BF16), v((64, 3072), BF16), v((32, 8, 8, 128), F32), v((64, nc), BF16),
            v((nz, 2, 128), F32), v((2 * ny * nx, 8, nz * 32), F32),
            v((12, 8, 128), F32), v((12, 8, 128), F32), v((12, 8, 128), F32), v((12, 8, 128), F32),
            v((12, 8, 128), F32),
            v((PER, 14, 8, 128), F32), v((PER, 14, 8, 128), F32), v((PER, 14, 8, 128), F32),
            v((14, 8, 128), F32), v((14, 8, 128), F32), v((14, 8, 128), F32),
            v((2, 96, 128), F32),
            pltpu.SemaphoreType.DMA((128,)), pltpu.SemaphoreType.DMA((128,)), pltpu.SemaphoreType.DMA((7,)),
        ]
        hbm = pl.BlockSpec(memory_space=pltpu.HBM)
        result = pl.pallas_call(
            functools.partial(kernel, ny, nx, nz),
            out_shape=jax.ShapeDtypeStruct((768, 128), F32),
            in_specs=[hbm] * 7,
            out_specs=pl.BlockSpec(memory_space=pltpu.VMEM),
            scratch_shapes=scratch,
            compiler_params=pltpu.CompilerParams(
                collective_id=0, has_side_effects=True, vmem_limit_bytes=64 * 1024 * 1024
            ),
            name="schwarz",
        )(
            loads.reshape(768, 128), iterate.reshape(768, 128), classes.reshape(32, 128), stiffness, density,
            basis.reshape(3072, 128), coarse_inverse,
        )
        return result.reshape(iterate.shape)

    field = P(None, None, "gx", "gy", "gz")
    return jax.shard_map(
        step,
        mesh=mesh,
        in_specs=(field, field, P("gx", "gy", "gz"), P(), P(), field, P(("gx", "gy", "gz"), None)),
        out_specs=field,
        check_vma=False,
    )
```

```python
import functools

import jax
import jax.numpy as jnp
from jax import lax
from jax.experimental import pallas as pl
from jax.experimental.pallas import tpu as pltpu
from jax.sharding import PartitionSpec as P

MESH = pl.DeviceIdType.MESH
F32, BF16, I32 = jnp.float32, jnp.bfloat16, jnp.int32
FIELDS = 24
CHUNKS, PER = 4, 6
COUPLING, DAMPING = 0.1, 0.7
NT = (((1,), (1,)), ((), ()))


def lookup(classes, table):
    found = jnp.zeros(classes.shape, F32)
    for k in range(8):
        found = found + jnp.where(classes == k, table[k], 0.0)
    return found


def halves(v):
    high = v.astype(BF16)
    return high, (v - high.astype(F32)).astype(BF16)


def iota(shape, axis):
    return lax.broadcasted_iota(I32, shape, axis)


def beside_x(v, axis):
    row = iota(v.shape, axis)
    return jnp.where(row == 0, 0.0, pltpu.roll(v, 1, axis)) + jnp.where(row == 7, 0.0, pltpu.roll(v, 7, axis))


def kernel(
    ny, nx, nz, loads, iterate, classes, stiffness_in, density_in, basis, cinv, acc,
    it, ld, cls, stiffness, density, bas, ci, res, iys, iyr, ixs, ixr, izs, izr, cbox, czs, czr, box, ys, yr,
    zs, zr, bh, bl, bf, wide, c2, g1, g2, sbox, wbox, bbox, zw, zb, ga, gb, gc, za, zc, zd, vy,
    ss, rs, ls,
):
    gx, gy, gz = lax.axis_index("gx"), lax.axis_index("gy"), lax.axis_index("gz")
    half = nz // 2
    py, core, px, pz = gx // 2, gx % 2, gy // 2, (gy % 2) * half + gz

    def chip(x, y, z, c):
        return (y * 2 + c, x * 2 + z // half, z % half)

    steps = {
        "gx": ((gx - 1, gy, gz), gx > 0, (gx + 1, gy, gz), gx < 2 * ny - 1),
        "gy": ((gx, gy - 1, gz), gy > 0, (gx, gy + 1, gz), gy < 2 * nx - 1),
        "gz": ((gx, gy, gz - 1), gz > 0, (gx, gy, gz + 1), gz < half - 1),
    }
    count = [0]
    pending = []

    def exchange(axis, low_src, low_dst, high_src, high_dst):
        lower, has_lower, upper, has_upper = steps[axis]
        i = count[0]
        count[0] += 2
        down = pltpu.make_async_remote_copy(low_src, low_dst, ss.at[i], rs.at[i], lower, MESH)
        up = pltpu.make_async_remote_copy(high_src, high_dst, ss.at[i + 1], rs.at[i + 1], upper, MESH)
        pl.when(has_lower)(down.start)
        pl.when(has_upper)(up.start)

        def sent():
            pl.when(has_lower)(down.wait_send)
            pl.when(has_upper)(up.wait_send)

        def arrived():
            pl.when(has_upper)(down.wait_recv)
            pl.when(has_lower)(up.wait_recv)

        pending.append(sent)
        return arrived

    local = [
        pltpu.make_async_copy(a, b, ls.at[i])
        for i, (a, b) in enumerate(
            (
                (iterate, it), (classes, cls), (loads, ld), (basis, bas), (cinv, ci),
                (stiffness_in, stiffness), (density_in, density),
            )
        )
    ]
    for i in (0, 1, 5, 6, 2):
        local[i].start()

    barrier = pltpu.get_barrier_semaphore()
    high_half = gy % 2
    across_gx = jnp.where(core == 1, gx < 2 * ny - 1, gx > 0)
    across_gy = jnp.where(high_half == 1, gy < 2 * nx - 1, gy > 0)
    for there, to in ((across_gx, (gx + 2 * core - 1, gy, gz)), (across_gy, (gx, gy + 2 * high_half - 1, gz))):
        pl.when(there)(functools.partial(pl.semaphore_signal, barrier, inc=1, device_id=to, device_id_type=MESH))

    def greet_line(k, carry):
        pl.semaphore_signal(barrier, inc=1, device_id=chip(px, py, lax.rem(pz + k, nz), core), device_id_type=MESH)
        return carry

    lax.fori_loop(1, nz, greet_line, 0)

    def other(p, sign):
        dx, dy = p // ny, lax.rem(p, ny)
        return lax.rem(px + sign * dx + nx, nx), lax.rem(py + sign * dy + ny, ny)

    def greet_plane(p, carry):
        x, y = other(p, 1)
        pl.semaphore_signal(barrier, inc=1, device_id=chip(x, y, pz, core), device_id_type=MESH)
        return carry

    lax.fori_loop(1, nx * ny, greet_plane, 0)
    twin = chip(px, py, pz, 1 - core)
    pl.semaphore_signal(barrier, inc=1, device_id=twin, device_id_type=MESH)

    lane8 = iota((8, 128), 1)
    zero8 = jnp.zeros((8, 128), F32)

    def clear(*views):
        def store():
            for ref, index in views:
                view = ref.at[index]
                view[...] = jnp.zeros(view.shape, ref.dtype)

        return store

    everything = slice(None)
    for side in range(2):
        layers = slice(10 * side, 10 * side + 2)
        planes = slice(6 * side, 6 * side + 2)
        missing = {axis: jnp.logical_not(step[1 + 2 * side]) for axis, step in steps.items()}
        pl.when(missing["gy"])(
            clear((iyr, side), (cbox, (layers, slice(2, 6))), (box, (everything, layers, slice(2, 6))))
        )
        pl.when(missing["gx"])(
            clear((ixr, side), (cbox, (everything, planes)), (box, (everything, everything, planes)))
        )
        pl.when(missing["gz"])(clear((izr, side), (czr, side), (zr, (everything, side))))

    local[0].wait()
    iys[0] = it[pl.ds(0, 96, stride=8), :]
    iys[1] = it[pl.ds(7, 96, stride=8), :]

    peers = nz - 1 + nx * ny - 1 + 1 + across_gx.astype(I32) + across_gy.astype(I32)
    pl.semaphore_wait(barrier, peers)

    it_y = exchange("gy", iys.at[0], iyr.at[1], iys.at[1], iyr.at[0])
    local[1].wait()
    for y in range(8):
        cbox[y + 2, 2:6] = cls[pl.ds(y, 4, stride=8), :] + 1

    cls_y = exchange("gy", cbox.at[2:4, 2:6], cbox.at[10:12, 2:6], cbox.at[8:10, 2:6], cbox.at[0:2, 2:6])

    def pack_iterate(f, carry):
        low, high = carry
        start = pl.multiple_of(f * 32, 32)
        ixs[0, f] = it[pl.ds(start, 8), :]
        ixs[1, f] = it[pl.ds(start + 24, 8), :]
        for x in range(4):
            v = it[pl.ds(start + x * 8, 8), :]
            t = x * 32 + f
            low = jnp.where(lane8 == t, pltpu.roll(v, t, 1), low)
            high = jnp.where(lane8 == t, pltpu.roll(v, t + 1, 1), high)
        return low, high

    low, high = lax.fori_loop(0, FIELDS, pack_iterate, (zero8, zero8), unroll=2)
    izs[0] = low
    izs[1] = high
    it_x = exchange("gx", ixs.at[0], ixr.at[1], ixs.at[1], ixr.at[0])
    it_z = exchange("gz", izs.at[0], izr.at[1], izs.at[1], izr.at[0])

    for i in (3, 4):
        local[i].start()
    acc[...] = it[...]
    for ref in (ga, gb, gc):
        ref[:, 0] = jnp.zeros((PER, 8, 128), F32)
        ref[:, 13] = jnp.zeros((PER, 8, 128), F32)
    for ref in (za, zc, zd):
        ref[0] = zero8
        ref[13] = zero8

    local[5].wait()
    local[6].wait()
    local[2].wait()

    def own_class(x):
        return cls[pl.ds(x * 8, 8), :]

    stiff_own = jnp.stack([lookup(own_class(x), stiffness) for x in range(4)])
    mass_own = jnp.stack([lookup(own_class(x), density) for x in range(4)])
    diag_own = 6.0 * stiff_own + mass_own - COUPLING * stiff_own

    it_x()
    it_z()

    def own_residual(col, carry):
        start = pl.multiple_of(col * 96, 96)
        u = it[pl.ds(start, 96), :].reshape(3, 4, 8, 128)
        lower = ixr[0, pl.ds(col * 3, 3)][:, None]
        upper = ixr[1, pl.ds(col * 3, 3)][:, None]
        near = jnp.concatenate([lower, u[:, :3]], 1) + jnp.concatenate([u[:, 1:], upper], 1)
        near = near + beside_x(u, 2)
        fill_low, fill_high = [], []
        for c in range(3):
            for x in range(4):
                t = x * 32 + col * 3 + c
                fill_low.append(pltpu.roll(izr[0], lax.rem(128 - t, 128), 1))
                fill_high.append(pltpu.roll(izr[1], 127 - t, 1))
        lane = iota(u.shape, 3)
        near = near + jnp.where(lane == 0, jnp.stack(fill_low).reshape(u.shape), pltpu.roll(u, 1, 3))
        near = near + jnp.where(lane == 127, jnp.stack(fill_high).reshape(u.shape), pltpu.roll(u, 127, 3))
        total = (u[0] + u[1] + u[2])[None]
        r = ld[pl.ds(start, 96), :].reshape(3, 4, 8, 128)
        r = r - diag_own[None] * u + stiff_own[None] * (near - COUPLING * total)
        res[pl.ds(start, 96), :] = r.reshape(96, 128)
        return carry

    lax.fori_loop(0, 8, own_residual, 0)

    def pack_rows(f, carry):
        for side in range(2):
            for layer in range(2):
                ys[side, f, layer * 4 : layer * 4 + 4] = res[pl.ds(f * 32 + side * 6 + layer, 4, stride=8), :]
        return carry

    lax.fori_loop(0, FIELDS, pack_rows, 0, unroll=2)
    res_y = {}

    def send_rows(ch):
        fs = pl.ds(ch * PER, PER)
        res_y[ch] = exchange("gy", ys.at[0, fs], yr.at[1, fs], ys.at[1, fs], yr.at[0, fs])

    send_rows(0)
    send_rows(1)
    send_rows(2)

    local[3].wait()

    def prepare_basis(k, carry):
        for cx in range(12):
            v = jnp.concatenate([bas[pl.ds((k * 4 + i) * 96 + cx * 8, 8), :] for i in range(4)], 0)
            rows = pl.ds(pl.multiple_of(k * 32, 32), 32)
            bh[rows, cx * 128 : cx * 128 + 128], bl[rows, cx * 128 : cx * 128 + 128] = halves(v)
        return carry

    lax.fori_loop(0, 8, prepare_basis, 0)
    for side in range(2):
        for cx in range(12):
            at = slice((side * 12 + cx) * 128, (side * 12 + cx) * 128 + 128)
            bf[0:32, at], bf[32:64, at] = halves(bas[pl.ds(cx * 8 + side * 7, 32, stride=96), :])

    def two(v):
        hi, lo = halves(v)
        return jnp.concatenate([hi, lo], 0)

    def coefficients(k, total):
        v = jnp.concatenate(
            [
                jnp.concatenate([res[pl.ds(col * 96 + (k * 2 + i) * 8, 8), :] for col in range(8)], 0)
                for i in range(2)
            ],
            1,
        )
        at = pl.ds(pl.multiple_of(k * 256, 256), 256)
        hi, lo = halves(v)
        total = total + lax.dot_general(hi, bh[:, at], NT, preferred_element_type=F32)
        total = total + lax.dot_general(lo, bh[:, at], NT, preferred_element_type=F32)
        return total + lax.dot_general(hi, bl[:, at], NT, preferred_element_type=F32)

    pairs = lax.fori_loop(0, 6, coefficients, jnp.zeros((64, 256), F32), unroll=6)
    equal = iota((64, 256), 0) % 8 == iota((64, 256), 1) % 8
    sums = jnp.sum(jnp.where(equal, pairs, 0.0).reshape(8, 8, 256), 1)
    fold = (iota((256, 128), 0) // 8 == iota((256, 128), 1)).astype(BF16)
    folded = jnp.dot(two(sums), fold, preferred_element_type=F32)
    coeff = folded[0:8] + folded[8:16]

    local[4].wait()

    def prepare_coarse(k, carry):
        at = pl.ds(pl.multiple_of(k * 512, 512), 512)
        hi, lo = halves(ci[:, at])
        c2[0:32, at] = hi
        c2[32:64, at] = lo
        return carry

    lax.fori_loop(0, ci.shape[1] // 512, prepare_coarse, 0, unroll=2)

    cls_y()
    cls_x = exchange("gx", cbox.at[:, 2:4], cbox.at[:, 6:8], cbox.at[:, 4:6], cbox.at[:, 0:2])

    it_y()
    parts = []
    for side in range(2):
        row = cls[pl.ds(side * 7, 4, stride=8), :]
        stiff = lookup(jnp.concatenate([row, row], 0), stiffness)
        vy[side] = (iyr[side].reshape(12, 8, 128) * stiff[None]).reshape(96, 128)
    for side in range(2):
        for cx in range(12):
            parts.append(vy[side, pl.ds(cx, 8, stride=12), :])
    faces = lax.dot_general(two(jnp.concatenate(parts, 1)), bf[...], NT, preferred_element_type=F32)

    def quarters(v):
        v = v[0:8] + v[8:16]
        v = v[:, 0:32] + v[:, 32:64]
        return jnp.concatenate([v, jnp.zeros((8, 96), F32)], 1)

    mine = coeff + quarters(faces)
    packed = zero8
    for q in range(4):
        v = pltpu.roll(mine, 32 * q, 1) if q else mine
        v = pltpu.roll(v, 8 - q, 0) if q else v
        packed = jnp.where(lane8 // 32 == q, v, packed)
    g1[pz, 0:1] = packed[0:1]
    g1[pz, 1:2] = packed[4:5]
    line = count[0]
    count[0] += nz
    plane = count[0]
    count[0] += nx * ny
    twins = count[0]
    count[0] += nx * ny

    def along_line(k):
        to = chip(px, py, lax.rem(pz + k, nz), core)
        return pltpu.make_async_remote_copy(g1.at[pz], g1.at[pz], ss.at[line + k], rs.at[line + k], to, MESH)

    def start_line(k, carry):
        along_line(k).start()
        return carry

    lax.fori_loop(1, nz, start_line, 0)
    send_rows(3)
    for side in range(2):
        at = pl.ds(side * 7, 96, stride=8)
        res[at, :] = res[at, :] + vy[side]

    cls_x()
    low = jnp.zeros((8, 128), I32)
    high = jnp.zeros((8, 128), I32)
    for y in range(12):
        mask = lane8 // 2 == y
        low = jnp.where(mask, pltpu.roll(cbox[y], 2 * y, 1), low)
        high = jnp.where(mask, pltpu.roll(cbox[y], 2 * y + 2, 1), high)
    czs[0] = low
    czs[1] = high
    cls_z = exchange("gz", czs.at[0], czr.at[1], czs.at[1], czr.at[0])

    def own_rows(f, carry):
        for y in range(8):
            box[f, y + 2, 2:6] = res[pl.ds(f * 32 + y, 4, stride=8), :]
        return carry

    lax.fori_loop(0, FIELDS, own_rows, 0, unroll=2)
    own_x = exchange("gx", box.at[:, 2:10, 2:4], box.at[:, 2:10, 6:8], box.at[:, 2:10, 4:6], box.at[:, 2:10, 0:2])


    def z_lanes(low, high, t, width):
        odd = lane8 % 2 == 1
        low, high = pltpu.roll(low, (128 - t) % 128, 1), pltpu.roll(high, (128 - t) % 128, 1)
        inner = jnp.where(odd, low, high)
        outer = jnp.where(odd, pltpu.roll(low, 1, 1), pltpu.roll(high, 127, 1))
        zero = jnp.zeros_like(inner)
        return jnp.where(lane8 < width, inner, zero) + pltpu.roll(jnp.where(lane8 < width, outer, zero), 64, 1)

    cls_z()

    def factors(shifted):
        inside = shifted > 0
        stiff = lookup(shifted - 1, stiffness)
        mass = lookup(shifted - 1, density)
        weight = jnp.where(inside, DAMPING / jnp.where(inside, 6.0 * stiff + mass - COUPLING * stiff, 1.0), 0.0)
        return stiff, weight

    def box_factors(y, carry):
        stiff, weight = factors(cbox[y])
        sbox[y] = stiff
        wbox[y] = weight
        bbox[y] = stiff * weight
        spread = z_lanes(czr[0], czr[1], 2 * y, 2)
        pair = spread + pltpu.roll(spread, 2, 1)
        spread = pair + pltpu.roll(pair, 4, 1) + pltpu.roll(pair, 8, 1)
        stiff, weight = factors(spread)
        zw[y] = weight
        zb[y] = stiff * weight
        return carry

    lax.fori_loop(0, 12, box_factors, 0, unroll=6)

    res_x, res_z = {}, {}

    def rows_arrive(ch):
        res_y[ch]()
        fs = pl.ds(ch * PER, PER)
        _, has_lower, _, has_upper = steps["gy"]

        @pl.when(has_lower)
        def _():
            for f in range(ch * PER, ch * PER + PER):
                v = yr[0, f]
                box[f, 0, 2:6] = v[0:4]
                box[f, 1, 2:6] = v[4:8] + sbox[1, 2:6] * iys[0, f * 4 : f * 4 + 4]

        @pl.when(has_upper)
        def _():
            for f in range(ch * PER, ch * PER + PER):
                v = yr[1, f]
                box[f, 10, 2:6] = v[0:4] + sbox[10, 2:6] * iys[1, f * 4 : f * 4 + 4]
                box[f, 11, 2:6] = v[4:8]

        first = exchange("gx", box.at[fs, 0:2, 2:4], box.at[fs, 0:2, 6:8], box.at[fs, 0:2, 4:6], box.at[fs, 0:2, 0:2])
        second = exchange(
            "gx", box.at[fs, 10:12, 2:4], box.at[fs, 10:12, 6:8], box.at[fs, 10:12, 4:6], box.at[fs, 10:12, 0:2]
        )
        res_x[ch] = (first, second)

    def planes_arrive(ch):
        if ch == 0:
            own_x()
        for arrived in res_x[ch]:
            arrived()
        lane = iota((12, 8, 128), 2)
        low = jnp.zeros((12, 8, 128), F32)
        high = jnp.zeros((12, 8, 128), F32)
        for i in range(PER):
            v = box[ch * PER + i]
            mask = lane // 2 == i
            low = jnp.where(mask, pltpu.roll(v, 2 * i, 2) if i else v, low)
            high = jnp.where(mask, pltpu.roll(v, 2 * i + 2, 2), high)
        for side, v in enumerate((low, high)):
            first, second = zero8, zero8
            for y in range(12):
                t = (y % 10) * 12
                w = pltpu.roll(v[y], t, 1) if t else v[y]
                if y < 10:
                    first = first + w
                else:
                    second = second + w
            zs[ch, side, 0] = first
            zs[ch, side, 1] = second
        res_z[ch] = exchange("gz", zs.at[ch, 0], zr.at[ch, 1], zs.at[ch, 1], zr.at[ch, 0])

    def sweep(src, zsrc, dst, zdst, y):
        e, z = src[:, y], zsrc[y]
        lane, lane6 = lane8, iota((PER, 8, 128), 2)
        near = src[:, y - 1] + src[:, y + 1] + beside_x(e, 1)
        fill = jnp.stack([pltpu.roll(z, 127 - 2 * i, 1) for i in range(PER)])
        near = near + jnp.where(lane6 == 0, fill, pltpu.roll(e, 1, 2))
        near = near + jnp.where(lane6 == 127, fill, pltpu.roll(e, 127, 2))
        totals = jnp.stack([e[0] + e[1] + e[2]] * 3 + [e[3] + e[4] + e[5]] * 3)
        dst_value = ga[:, y] + (1.0 - DAMPING) * e + bbox[y - 1][None] * (near - COUPLING * totals)
        if zdst is not None:
            dst[:, y] = dst_value
            push = jnp.zeros((8, 128), F32)
            for i in range(PER):
                push = jnp.where(lane // 2 == i, pltpu.roll(e[i], 2 * i + 1, 1), push)
            znear = zsrc[y - 1] + zsrc[y + 1] + beside_x(z, 0) + push + pltpu.roll(z, 64, 1)
            two_on, four_on = pltpu.roll(z, 126, 1), pltpu.roll(z, 124, 1)
            two_back, four_back = pltpu.roll(z, 2, 1), pltpu.roll(z, 4, 1)
            comp = ((lane % 64) // 2) % 3
            rest = jnp.where(
                comp == 0, two_on + four_on, jnp.where(comp == 1, two_on + two_back, two_back + four_back)
            )
            zdst[y] = za[y] + (1.0 - DAMPING) * z + zb[y - 1] * (znear - COUPLING * (z + rest))
        return dst_value

    def sweeps(ch):
        res_z[ch]()

        def start(y, carry):
            ga[:, y + 1] = box[pl.ds(ch * PER, PER), y] * wbox[y][None]
            return carry

        lax.fori_loop(0, 12, start, 0)
        for y in range(12):
            t = (y % 10) * 12
            z = z_lanes(zr[ch, 0, y // 10], zr[ch, 1, y // 10], t, 2 * PER)
            za[y + 1] = z * zw[y]

        def first(y, carry):
            sweep(ga, za, gb, zc, y)
            return carry

        lax.fori_loop(1, 13, first, 0, unroll=12)

        def second(y, carry):
            sweep(gb, zc, gc, zd, y)
            return carry

        lax.fori_loop(2, 12, second, 0, unroll=10)

        def third(y, carry):
            v = sweep(gc, zd, None, None, y)
            for i in range(PER):
                at = pl.ds((ch * PER + i) * 32 + y - 3, 4, stride=8)
                acc[at, :] = acc[at, :] + v[i, 2:6]
            return carry

        lax.fori_loop(3, 11, third, 0, unroll=8)

    def block(x, y, c):
        return (y * 2 + c) * nx + x

    def along_plane(p):
        x, y = other(p, 1)
        b = block(px, py, core)
        return pltpu.make_async_remote_copy(
            g2.at[b], g2.at[b], ss.at[plane + p], rs.at[plane + p], chip(x, y, pz, core), MESH
        )

    def to_twin(p):
        x, y = other(p, -1)
        b = block(x, y, core)
        return pltpu.make_async_remote_copy(g2.at[b], g2.at[b], ss.at[twins + p], rs.at[twins + p], twin, MESH)

    def line_arrives():
        def arrive(k, carry):
            along_line(k).wait_recv()
            return carry

        lax.fori_loop(1, nz, arrive, 0)
        groups = nz // 4
        rows = g1[...]
        upper = jnp.broadcast_to(rows[:, 0:1], (nz, 8, 128))
        lower = jnp.broadcast_to(rows[:, 1:2], (nz, 8, 128))
        both = jnp.where(iota((nz, 8, 128), 1) < 4, upper, lower).reshape(groups, 4, 8, 128)
        lane, sub = iota((groups, 8, 128), 2) // 32, iota((groups, 8, 128), 1) % 4
        spread = jnp.zeros((groups, 8, 128), F32)
        for zz in range(4):
            for q in range(4):
                t = 32 * ((zz - q) % 4)
                v = both[:, zz]
                v = pltpu.roll(v, t, 2) if t else v
                spread = jnp.where((lane == zz) & (sub == q), v, spread)
        b = block(px, py, core)
        g2[b] = jnp.concatenate([spread[i] for i in range(groups)], 1)

        def start(p, carry):
            along_plane(p).start()
            return carry

        lax.fori_loop(1, nx * ny, start, 0)
        to_twin(0).start()

    width = nz * 32

    def times_blocks(c, total):
        def add(p, total):
            x, y = other(p, -1)
            b = block(x, y, c)
            at = pl.ds(pl.multiple_of(b * width, width), width)
            return total + lax.dot_general(two(g2[b]), c2[:, at], NT, preferred_element_type=F32)

        return lax.fori_loop(0, nx * ny, add, total, unroll=nx * ny)

    def plane_arrives():
        def arrive(p, carry):
            along_plane(p).wait_recv()
            to_twin(p).start()
            return carry

        lax.fori_loop(1, nx * ny, arrive, 0)
        return times_blocks(core, jnp.zeros((16, 64), F32))

    def twins_arrive(total):
        def arrive(p, carry):
            to_twin(p).wait_recv()
            return carry

        lax.fori_loop(0, nx * ny, arrive, 0)
        total = times_blocks(1 - core, total)
        solved = quarters(total)
        for j in range(32):
            column = jnp.broadcast_to(solved[:, j : j + 1], (8, 128))
            wide[j] = jnp.broadcast_to(column[:, None], (8, 8, 128))

        def correct(k, carry):
            def add(j, sums):
                parts = [bas[pl.ds(pl.multiple_of(j * 96 + k * 16 + i * 8, 8), 8), :] for i in range(2)]
                out = []
                for col in range(8):
                    factor = wide[j, col]
                    out += [sums[2 * col + i] + factor * parts[i] for i in range(2)]
                return tuple(out)

            sums = lax.fori_loop(0, 32, add, (zero8,) * 16, unroll=8)
            for col in range(8):
                for i in range(2):
                    rows = pl.ds(pl.multiple_of(col * 96 + k * 16 + i * 8, 8), 8)
                    acc[rows, :] = acc[rows, :] + sums[2 * col + i]
            return carry

        lax.fori_loop(0, 6, correct, 0)

    rows_arrive(0)
    rows_arrive(1)
    line_arrives()
    rows_arrive(2)
    rows_arrive(3)
    planes_arrive(0)
    planes_arrive(1)
    planes_arrive(2)
    planes_arrive(3)
    sweeps(0)
    sweeps(1)
    total = plane_arrives()
    sweeps(2)
    sweeps(3)
    twins_arrive(total)

    for sent in pending:
        sent()

    def all_sent(k, carry):
        along_line(k).wait_send()
        return carry

    lax.fori_loop(1, nz, all_sent, 0)

    def all_sent_plane(p, carry):
        along_plane(p).wait_send()
        to_twin(p).wait_send()
        return carry

    to_twin(0).wait_send()
    lax.fori_loop(1, nx * ny, all_sent_plane, 0)


def solution(mesh):
    ny, nx, nz = mesh.shape["gx"] // 2, mesh.shape["gy"] // 2, mesh.shape["gz"] * 2
    nc = 2 * ny * nx * nz * 32

    def step(loads, iterate, classes, stiffness, density, basis, coarse_inverse):
        v = pltpu.VMEM
        scratch = [
            v((768, 128), F32), v((768, 128), F32), v((32, 128), I32),
            pltpu.SMEM((8,), F32), pltpu.SMEM((8,), F32), v((3072, 128), F32),
            v((32, nc), F32), v((768, 128), F32),
            v((2, 96, 128), F32), v((2, 96, 128), F32), v((2, FIELDS, 8, 128), F32), v((2, FIELDS, 8, 128), F32),
            v((2, 8, 128), F32), v((2, 8, 128), F32),
            v((12, 8, 128), I32), v((2, 8, 128), I32), v((2, 8, 128), I32),
            v((FIELDS, 12, 8, 128), F32), v((2, FIELDS, 8, 128), F32), v((2, FIELDS, 8, 128), F32),
            v((CHUNKS, 2, 2, 8, 128), F32), v((CHUNKS, 2, 2, 8, 128), F32),
            v((256, 1536), BF16), v((256, 1536), BF16), v((64, 3072), BF16), v((32, 8, 8, 128), F32), v((64, nc), BF16),
            v((nz, 2, 128), F32), v((2 * ny * nx, 8, nz * 32), F32),
            v((12, 8, 128), F32), v((12, 8, 128), F32), v((12, 8, 128), F32), v((12, 8, 128), F32),
            v((12, 8, 128), F32),
            v((PER, 14, 8, 128), F32), v((PER, 14, 8, 128), F32), v((PER, 14, 8, 128), F32),
            v((14, 8, 128), F32), v((14, 8, 128), F32), v((14, 8, 128), F32),
            v((2, 96, 128), F32),
            pltpu.SemaphoreType.DMA((128,)), pltpu.SemaphoreType.DMA((128,)), pltpu.SemaphoreType.DMA((7,)),
        ]
        hbm = pl.BlockSpec(memory_space=pltpu.HBM)
        result = pl.pallas_call(
            functools.partial(kernel, ny, nx, nz),
            out_shape=jax.ShapeDtypeStruct((768, 128), F32),
            in_specs=[hbm] * 7,
            out_specs=pl.BlockSpec(memory_space=pltpu.VMEM),
            scratch_shapes=scratch,
            compiler_params=pltpu.CompilerParams(
                collective_id=0, has_side_effects=True, vmem_limit_bytes=64 * 1024 * 1024
            ),
            name="schwarz",
        )(
            loads.reshape(768, 128), iterate.reshape(768, 128), classes.reshape(32, 128), stiffness, density,
            basis.reshape(3072, 128), coarse_inverse,
        )
        return result.reshape(iterate.shape)

    field = P(None, None, "gx", "gy", "gz")
    return jax.shard_map(
        step,
        mesh=mesh,
        in_specs=(field, field, P("gx", "gy", "gz"), P(), P(), field, P(("gx", "gy", "gz"), None)),
        out_specs=field,
        check_vma=False,
    )
```
